32 devices in a mesh: ctx: 8 (over z, y), fsdp: 4 (over x, core).
Axes of the slice: x: 2, y: 2, z: 4, core: 2. Of those that a mesh axis runs over, the one named last changes fastest.
Arguments:
- tokens: bfloat16 [4, 2048, 768], P('fsdp', 'ctx'), may hold values from -6 to 6
- encoded: bfloat16 [4, 1024, 768], P('fsdp', 'ctx'), may hold values from -6 to 6
- cotangent: bfloat16 [4, 2048, 768], P('fsdp', 'ctx'), may hold values from -6 to 6
- w_self: bfloat16 [768, 3072], P('fsdp'), may hold values from -1 to 1
- w_cross: bfloat16 [768, 3072], P('fsdp'), may hold values from -1 to 1
- w_ffn: bfloat16 [768, 6144], P('fsdp'), may hold values from -1 to 1
- gains: bfloat16 [3, 768], P(None, 'fsdp'), may hold values from 0.5 to 1.5
- table: bfloat16 [32, 12], P('fsdp'), may hold values from -4 to 4
- bucket_ids: int32 [2048], replicated, may hold values from 0 to 31, as said below
- block_order: int32 [16], replicated, may hold values from 0 to 15, each once
Outputs:
- output: bfloat16 [4, 2048, 768], P('fsdp', 'ctx')
- grad_tokens: bfloat16 [4, 2048, 768], P('fsdp', 'ctx')
- grad_encoded: bfloat16 [4, 1024, 768], P('fsdp', 'ctx')
- grad_w_self: float32 [768, 3072], P('fsdp')
- grad_w_cross: float32 [768, 3072], P('fsdp')
- feedforward_weight_gradient: float32 [768, 6144], P('fsdp')
- grad_gains: float32 [3, 768], P(None, 'fsdp')
- grad_table: float32 [32, 12], P('fsdp')
The draws below stay inside these ranges and needn't reach their ends.
Inputs may be any that keep to these rules, and one draw needn't show every extreme that they name: `bucket_ids`: nondecreasing in the distance; distances 0 to 7 have buckets 0 to 7, and the buckets above grow about logarithmically with the distance. Each block number once; ctx device c holds block block_order[2 * c] in its first 128 rows and block_order[2 * c + 1] in the rest.
All inputs are finite; a program needn't handle non-finite values.
Results may differ from the reference program's by a relative error of at most 0.04.
Values may be sent and summed in bfloat16 or wider, within the bound.
No kernel may reach another device: no remote copies, remote signals or barrier semaphores. Data moves between devices by JAX's collectives and lax.ppermute only.
A program may use at most 192 MiB of HBM per device.

```python
import math
import jax
import jax.numpy as jnp
import numpy as np
from jax import lax

D = 768
H = 12
DH = 64
FF = 2048
BUCKETS = 32
ENC = 1024
SEQ = 2048
NSEQ = 4
BLK = 128
BLOCKS = 16


def column_scales(widths, factors):
    return jnp.concatenate([jnp.full((column_width,), factor_value, jnp.float32) for column_width, factor_value in zip(widths, factors)])


def draw_w_self(key, part):
    key = jax.random.fold_in(key, 3)
    scales = column_scales((D, D, D, D), (0.5, 0.5, 1.0, 4.0)) / math.sqrt(D)
    samples = jnp.clip(jax.random.normal(key, (D, 4 * D), jnp.float32), -6.0, 6.0)
    return jnp.clip(samples * scales[None, :], -1.0, 1.0).astype(jnp.bfloat16)


def draw_w_cross(key, part):
    key = jax.random.fold_in(key, 5)
    scales = column_scales((D, D, D, D), (0.5, 0.5, 1.0, 3.0)) / math.sqrt(D)
    samples = jnp.clip(jax.random.normal(key, (D, 4 * D), jnp.float32), -6.0, 6.0)
    return jnp.clip(samples * scales[None, :], -1.0, 1.0).astype(jnp.bfloat16)


def draw_w_ffn(key, part):
    key = jax.random.fold_in(key, 7)
    scales = column_scales((FF, FF, FF), (1.0 / math.sqrt(D), 1.0 / math.sqrt(D), 1.5 / math.sqrt(FF)))
    samples = jnp.clip(jax.random.normal(key, (D, 3 * FF), jnp.float32), -6.0, 6.0)
    return jnp.clip(samples * scales[None, :], -1.0, 1.0).astype(jnp.bfloat16)


def draw_bucket_ids(key, part):
    key = jax.random.fold_in(key, 11)
    levels = np.arange(1, BUCKETS)
    growth = np.floor(8.0 * (SEQ / 8.0) ** ((levels - 8) / (BUCKETS - 8.0)))
    base = np.where(levels < 8, levels, growth).astype(np.int32)
    jitter = jax.random.randint(key, (BUCKETS - 1,), 0, jnp.asarray(base // 4 + 1, jnp.int32))
    jitter = jnp.where(jnp.asarray(levels) >= 8, jitter, 0)
    steps_up = jnp.asarray(levels, jnp.int32)
    promoted_rows = lax.cummax(jnp.asarray(base, jnp.int32) + jitter - steps_up, axis=0) + steps_up
    thresholds = jnp.minimum(promoted_rows, SEQ - BUCKETS + steps_up)
    offsets = jnp.arange(SEQ, dtype=jnp.int32)
    return jnp.sum((offsets[:, None] >= thresholds[None, :]).astype(jnp.int32), axis=1).astype(jnp.int32)


def shard_levels(rng, extent, pieces, least, top_value):
    level, own = 1.0, jax.random.fold_in(rng, 6)
    for dim, shards_of in pieces:
        heights = jnp.exp(jax.random.uniform(jax.random.fold_in(own, dim), (shards_of,), jnp.float32, least / len(pieces), top_value / len(pieces)))
        level = level * jnp.repeat(heights, extent[dim] // shards_of).reshape([-1 if axis == dim else 1 for axis in range(len(extent))])
    return level


def normal_values(own_key, shape, deviation, most, split=(), kind=jnp.bfloat16):
    loudness = shard_levels(own_key, shape, split, -0.22, 0.18) if split else 1.0
    result = jax.random.normal(own_key, shape, jnp.float32) * deviation * loudness
    return jnp.minimum(jnp.maximum(result, -most), most).astype(kind)


def setup_inputs(seed: int = 0) -> dict:
    arg_keys = jax.random.split(jax.random.key(seed), 11)
    return {
        "tokens": normal_values(arg_keys[0], (NSEQ, SEQ, D), 1.0, 6.0, ((0, 4), (1, 8))),
        "encoded": normal_values(arg_keys[1], (NSEQ, ENC, D), 1.0, 6.0, ((0, 4), (1, 8))),
        "cotangent": normal_values(arg_keys[2], (NSEQ, SEQ, D), 1.0, 6.0, ((0, 4), (1, 8))),
        "w_self": draw_w_self(jax.random.fold_in(arg_keys[10], 71), 0),
        "w_cross": draw_w_cross(jax.random.fold_in(arg_keys[10], 71), 0),
        "w_ffn": draw_w_ffn(jax.random.fold_in(arg_keys[10], 71), 0),
        "gains": jnp.clip(1.0 + 0.1 * jax.random.normal(arg_keys[6], (3, D), jnp.float32), 0.5, 1.5).astype(jnp.bfloat16),
        "table": normal_values(arg_keys[7], (BUCKETS, H), 1.0, 4.0, ((0, 4),)),
        "bucket_ids": draw_bucket_ids(jax.random.fold_in(arg_keys[10], 71), 0),
        "block_order": jax.random.permutation(arg_keys[9], BLOCKS).astype(jnp.int32),
    }


HIGHEST = lax.Precision.HIGHEST
EPSILON = 1e-06
NEGATIVE = -1e+30

@jax.custom_vjp
def low(v):
    return lax.optimization_barrier(v.astype(jnp.bfloat16)).astype(jnp.float32)

@jax.custom_vjp
def low_back(v):
    return v

def low_keep(v):
    return (low(v), None)

def low_pass(kept, grad):
    return (grad,)

def back_keep(v):
    return (v, None)

def back_low(kept, grad):
    return (low(grad),)
low.defvjp(low_keep, low_pass)
low_back.defvjp(back_keep, back_low)

def round_both(values):
    return low(low_back(values))

def product(left, right):
    return jnp.dot(left, right, precision=HIGHEST)

def rms_norm(values, gain):
    return values * lax.rsqrt(lax.optimization_barrier(jnp.mean(values * values, axis=-1, keepdims=True)) + EPSILON) * gain

def attend(query_rows, key_rows, value_rows, extra, allowed):
    scores = jnp.einsum('qhd,khd->hqk', query_rows, key_rows, precision=HIGHEST) + extra
    scores = jnp.where(allowed, low_back(scores), NEGATIVE)
    weights = low(jax.nn.softmax(scores, axis=-1))
    mixed_rows = jnp.einsum('hqk,khd->qhd', weights, value_rows, precision=HIGHEST)
    return mixed_rows.reshape(query_rows.shape[0], D)

def one_sequence(tokens, encoded, w_self, w_cross, w_ffn, gains, table, bucket_ids, position):
    block_rows = math.gcd(SEQ, 512)
    block_count = SEQ // block_rows
    normed = low(rms_norm(tokens, gains[0]))
    query_rows = round_both(product(normed, w_self[:, :D])).reshape(SEQ, H, DH)
    key_rows = round_both(product(normed, w_self[:, D:2 * D])).reshape(SEQ, H, DH)
    value_rows = round_both(product(normed, w_self[:, 2 * D:3 * D])).reshape(SEQ, H, DH)
    offset_bias = table[bucket_ids]

    def self_block(operands):
        query_block, query_pos = operands
        offsets = query_pos[:, None] - position[None, :]
        extra = jnp.transpose(offset_bias[jnp.clip(offsets, 0, SEQ - 1)], (2, 0, 1))
        return attend(query_block, key_rows, value_rows, extra, (offsets >= 0)[None])
    attended = lax.map(jax.checkpoint(self_block), (query_rows.reshape(block_count, block_rows, H, DH), position.reshape(block_count, block_rows)))
    attended = round_both(attended.reshape(SEQ, D))
    after_one = tokens + low_back(product(attended, w_self[:, 3 * D:]))
    normed_two = low(rms_norm(after_one, gains[1]))
    cross_query = round_both(product(normed_two, w_cross[:, :D])).reshape(block_count, block_rows, H, DH)
    cross_keys = round_both(product(encoded, w_cross[:, D:2 * D])).reshape(ENC, H, DH)
    cross_values = round_both(product(encoded, w_cross[:, 2 * D:3 * D])).reshape(ENC, H, DH)

    def cross_block(query_block):
        return attend(query_block, cross_keys, cross_values, 0.0, True)
    cross_out = round_both(lax.map(jax.checkpoint(cross_block), cross_query).reshape(SEQ, D))
    after_two = after_one + low_back(product(cross_out, w_cross[:, 3 * D:]))
    normed_three = low(rms_norm(after_two, gains[2]))
    gate = low_back(product(normed_three, w_ffn[:, :FF]))
    upward = low_back(product(normed_three, w_ffn[:, FF:2 * FF]))
    mixed_rows = low(jax.nn.gelu(gate, approximate=True) * upward)
    return after_two + low_back(product(mixed_rows, w_ffn[:, 2 * FF:].T))

def reference(tokens, encoded, cotangent, w_self, w_cross, w_ffn, gains, table, bucket_ids, block_order):
    row_index = jnp.arange(SEQ, dtype=jnp.int32)
    position = (block_order[row_index // BLK] * BLK + row_index % BLK).astype(jnp.int32)

    def decoder_layer(token_all, encoded_all, self_all, cross_all, ffn_all, gain_all, table_all):

        def run_sequence(operands):
            return one_sequence(operands[0], operands[1], self_all, cross_all, ffn_all, gain_all, table_all, bucket_ids, position)
        return lax.map(run_sequence, (token_all, encoded_all))
    outputs, pullback = jax.vjp(decoder_layer, tokens.astype(jnp.float32), encoded.astype(jnp.float32), w_self.astype(jnp.float32), w_cross.astype(jnp.float32), w_ffn.astype(jnp.float32), gains.astype(jnp.float32), table.astype(jnp.float32))
    gradients = pullback(cotangent.astype(jnp.float32))
    return (outputs.astype(jnp.bfloat16), gradients[0].astype(jnp.bfloat16), gradients[1].astype(jnp.bfloat16), gradients[2], gradients[3], gradients[4], gradients[5], gradients[6])
```

```python
import functools

import jax
import jax.numpy as jnp
from jax import lax
from jax.experimental import pallas as pl
from jax.experimental.pallas import tpu as pltpu
from jax.sharding import PartitionSpec as P

NEGATIVE = -1e30
LANES = 128
VMEM_BYTES = 56 * 2**20


def dot(left, right):
    return lax.dot_general(
        left, right, (((1,), (0,)), ((), ())), preferred_element_type=jnp.float32
    )


def dot_t(left, right):
    return lax.dot_general(
        left, right, (((1,), (1,)), ((), ())), preferred_element_type=jnp.float32
    )


def t_dot(left, right):
    return lax.dot_general(
        left, right, (((0,), (0,)), ((), ())), preferred_element_type=jnp.float32
    )


def head_lanes(shape, head, head_size):
    lane = lax.broadcasted_iota(jnp.int32, shape, len(shape) - 1)
    return (lane >= head * head_size) & (lane < (head + 1) * head_size)


def only_head(values, head, head_size):
    return jnp.where(head_lanes(values.shape, head, head_size), values, jnp.zeros_like(values))


def tile_kernel(vector_ref, tile_ref):
    size = tile_ref.shape[-1]
    for head in range(vector_ref.shape[0]):
        for step in range(vector_ref.shape[1]):
            row = jnp.broadcast_to(
                vector_ref[head, step : step + 1, :], (size, 2 * size)
            )
            rolled = pltpu.roll(row, 0, 1, stride=1, stride_axis=0)
            tile_ref[head, step] = rolled[:, :size].astype(jnp.bfloat16)


def bias_tiles(vectors, group):
    head_count, steps, width = vectors.shape
    size = width // 2
    return pl.pallas_call(
        tile_kernel,
        grid=(head_count // group,),
        in_specs=[pl.BlockSpec((group, steps, width), lambda g: (g, 0, 0))],
        out_specs=pl.BlockSpec((group, steps, size, size), lambda g: (g, 0, 0, 0)),
        out_shape=jax.ShapeDtypeStruct((head_count, steps, size, size), jnp.bfloat16),
        compiler_params=pltpu.CompilerParams(vmem_limit_bytes=VMEM_BYTES),
        name="bias_tiles",
    )(vectors)


def forward_kernel(head_size, biased, *refs):
    if biased:
        place_ref, q_ref, k_ref, v_ref, tile_ref, out_ref, weight_ref, inverse_ref, score_ref = refs
    else:
        q_ref, k_ref, v_ref, out_ref, weight_ref, inverse_ref, score_ref = refs
    rows, key_total = q_ref.shape[0], k_ref.shape[0]
    group = q_ref.shape[1] // head_size
    piece = LANES
    out = jnp.zeros(q_ref.shape, jnp.float32)
    for head in range(group):
        query = only_head(q_ref[...], head, head_size)
        tops = [None] * (rows // piece)
        wide = 512
        for start in range(0, key_total, wide):
            scores = dot_t(query, k_ref[start : start + wide, :])
            for half in range(rows // piece):
                for part in range(wide // piece):
                    block = scores[
                        half * piece : (half + 1) * piece, part * piece : (part + 1) * piece
                    ]
                    key_block = start // piece + part
                    if biased:
                        place = place_ref[half * (key_total // piece) + key_block]
                        block = block + tile_ref[head, place].astype(jnp.float32)
                    score_ref[
                        half * piece : (half + 1) * piece,
                        key_block * piece : (key_block + 1) * piece,
                    ] = block
                    tops[half] = block if tops[half] is None else jnp.maximum(tops[half], block)
        top = jnp.concatenate([jnp.max(t, axis=1, keepdims=True) for t in tops], axis=0)
        total = jnp.zeros((rows, piece), jnp.float32)
        for start in range(0, key_total, piece):
            weights = jnp.exp(score_ref[:, start : start + piece] - top)
            total = total + weights
            weight_ref[head, :, start : start + piece] = weights.astype(jnp.bfloat16)
        inverse = 1.0 / jnp.sum(total, axis=1, keepdims=True)
        inverse_ref[head] = jnp.broadcast_to(inverse, (rows, LANES))
        mixed = dot(weight_ref[head], v_ref[...]) * inverse
        out = jnp.where(head_lanes(out.shape, head, head_size), mixed, out)
    out_ref[...] = out.astype(jnp.bfloat16)


def attention_forward(queries, key_values, head_size, tiles=None, places=None):
    rows, width = queries.shape
    key_total = key_values.shape[0]
    pairs = width // LANES
    group = LANES // head_size
    column = lambda shift: (lambda g, *_: (0, g + shift))
    in_specs = [
        pl.BlockSpec((rows, LANES), column(0)),
        pl.BlockSpec((key_total, LANES), column(0)),
        pl.BlockSpec((key_total, LANES), column(pairs)),
    ]
    operands = [queries, key_values, key_values]
    if tiles is not None:
        in_specs.append(
            pl.BlockSpec((group,) + tiles.shape[1:], lambda g, *_: (g, 0, 0, 0))
        )
        operands.append(tiles)
    grid_spec = pltpu.PrefetchScalarGridSpec(
        num_scalar_prefetch=0 if tiles is None else 1,
        grid=(pairs,),
        in_specs=in_specs,
        out_specs=[
            pl.BlockSpec((rows, LANES), column(0)),
            pl.BlockSpec((group, rows, key_total), lambda g, *_: (g, 0, 0)),
            pl.BlockSpec((group, rows, LANES), lambda g, *_: (g, 0, 0)),
        ],
        scratch_shapes=[pltpu.VMEM((rows, key_total), jnp.float32)],
    )
    heads = width // head_size
    return pl.pallas_call(
        functools.partial(forward_kernel, head_size, tiles is not None),
        grid_spec=grid_spec,
        out_shape=[
            jax.ShapeDtypeStruct((rows, width), jnp.bfloat16),
            jax.ShapeDtypeStruct((heads, rows, key_total), jnp.bfloat16),
            jax.ShapeDtypeStruct((heads, rows, LANES), jnp.float32),
        ],
        compiler_params=pltpu.CompilerParams(vmem_limit_bytes=VMEM_BYTES),
        cost_estimate=pl.CostEstimate(
            flops=8 * rows * key_total * width,
            bytes_accessed=2 * heads * rows * key_total + 4 * key_total * width,
            transcendentals=heads * rows * key_total,
        ),
        name="attention_forward",
    )(*(() if places is None else (places,)), *operands)


def backward_kernel(head_size, biased, *refs):
    if biased:
        (place_ref, q_ref, k_ref, v_ref, grad_ref, out_ref, weight_ref, inverse_ref,
         dq_ref, dkv_ref, dist_ref, ds_ref, sum_ref) = refs
    else:
        (q_ref, k_ref, v_ref, grad_ref, out_ref, weight_ref, inverse_ref,
         dq_ref, dkv_ref, ds_ref) = refs
    rows, key_total = q_ref.shape[0], k_ref.shape[0]
    group = q_ref.shape[1] // head_size
    piece = LANES
    wide = 512
    dq = jnp.zeros(q_ref.shape, jnp.float32)
    grads = grad_ref[...].astype(jnp.float32)
    deltas = grads * out_ref[...].astype(jnp.float32)
    if biased:
        sum_ref[...] = jnp.zeros_like(sum_ref)
    scaled_all = []
    for head in range(group):
        inverse = inverse_ref[head]
        scaled = only_head((grads * inverse).astype(jnp.bfloat16), head, head_size)
        scaled_all.append(scaled)
        delta = jnp.sum(only_head(deltas, head, head_size), axis=1, keepdims=True) * inverse
        for start in range(0, key_total, wide):
            grad_probs = dot_t(scaled, v_ref[start : start + wide, :])
            for half in range(rows // piece):
                for part in range(wide // piece):
                    lo = half * piece
                    at = start + part * piece
                    block = grad_probs[lo : lo + piece, part * piece : (part + 1) * piece]
                    weights = weight_ref[head, lo : lo + piece, at : at + piece]
                    change = weights.astype(jnp.float32) * (block - delta[lo : lo + piece])
                    ds_ref[head * rows + lo : head * rows + lo + piece, at : at + piece] = (
                        change.astype(jnp.bfloat16)
                    )
                    if biased:
                        place = place_ref[half * (key_total // piece) + at // piece]
                        sum_ref[head, place] += change
        mixed = dot(ds_ref[head * rows : (head + 1) * rows, :], k_ref[...])
        dq = jnp.where(head_lanes(dq.shape, head, head_size), mixed, dq)
    dq_ref[...] = dq.astype(jnp.bfloat16)
    queries = jnp.concatenate(
        [only_head(q_ref[...], head, head_size) for head in range(group)], axis=0
    )
    scaled_rows = jnp.concatenate(scaled_all, axis=0)
    for start in range(0, key_total, wide):
        dkv_ref[0, start : start + wide, :] = t_dot(
            ds_ref[:, start : start + wide], queries
        ).astype(jnp.bfloat16)
        weights = jnp.concatenate(
            [weight_ref[head, :, start : start + wide] for head in range(group)], axis=0
        )
        dkv_ref[1, start : start + wide, :] = t_dot(weights, scaled_rows).astype(
            jnp.bfloat16
        )
    if biased:
        steps = dist_ref.shape[1]
        down = lax.broadcasted_iota(jnp.int32, (piece, piece), 0)
        across = lax.broadcasted_iota(jnp.int32, (piece, piece), 1)
        flip = (down + across == piece - 1).astype(jnp.bfloat16)

        def fold(step, carry):
            for head in range(group):
                block = sum_ref[head, step]
                high = block.astype(jnp.bfloat16)
                low = (block - high.astype(jnp.float32)).astype(jnp.bfloat16)
                turned = dot(flip, high) + dot(flip, low)
                padded = jnp.concatenate([turned, jnp.zeros_like(turned)], axis=1)
                rolled = pltpu.roll(padded, piece + 1, 1, stride=1, stride_axis=0)
                dist_ref[head, pl.ds(step, 1), :] = jnp.sum(rolled, axis=0, keepdims=True)
            return carry

        lax.fori_loop(0, steps, fold, 0)


def attention_backward(
    queries, key_values, grads, outs, weights, inverses, head_size, places=None, steps=0
):
    rows, width = queries.shape
    key_total = key_values.shape[0]
    pairs = width // LANES
    group = LANES // head_size
    heads = width // head_size
    biased = places is not None
    column = lambda shift: (lambda g, *_: (0, g + shift))
    row_block = pl.BlockSpec((rows, LANES), column(0))
    key_block = pl.BlockSpec((key_total, LANES), column(0))
    out_specs = [row_block, pl.BlockSpec((2, key_total, LANES), lambda g, *_: (0, 0, g))]
    out_shape = [
        jax.ShapeDtypeStruct((rows, width), jnp.bfloat16),
        jax.ShapeDtypeStruct((2, key_total, width), jnp.bfloat16),
    ]
    scratch = [pltpu.VMEM((group * rows, key_total), jnp.bfloat16)]
    if biased:
        out_specs.append(pl.BlockSpec((group, steps, 2 * LANES), lambda g, *_: (g, 0, 0)))
        out_shape.append(jax.ShapeDtypeStruct((heads, steps, 2 * LANES), jnp.float32))
        scratch.append(pltpu.VMEM((group, steps + 1, LANES, LANES), jnp.float32))
    grid_spec = pltpu.PrefetchScalarGridSpec(
        num_scalar_prefetch=1 if biased else 0,
        grid=(pairs,),
        in_specs=[
            row_block,
            key_block,
            pl.BlockSpec((key_total, LANES), column(pairs)),
            row_block,
            row_block,
            pl.BlockSpec((group, rows, key_total), lambda g, *_: (g, 0, 0)),
            pl.BlockSpec((group, rows, LANES), lambda g, *_: (g, 0, 0)),
        ],
        out_specs=out_specs,
        scratch_shapes=scratch,
    )
    return pl.pallas_call(
        functools.partial(backward_kernel, head_size, biased),
        grid_spec=grid_spec,
        out_shape=out_shape,
        compiler_params=pltpu.CompilerParams(vmem_limit_bytes=VMEM_BYTES),
        cost_estimate=pl.CostEstimate(
            flops=16 * rows * key_total * width,
            bytes_accessed=2 * heads * rows * key_total + 8 * key_total * width,
            transcendentals=0,
        ),
        name="attention_backward",
    )(
        *((places,) if biased else ()),
        queries, key_values, key_values, grads, outs, weights, inverses,
    )


EPSILON = 1e-06


def row_norm(values, gain):
    return values * lax.rsqrt(jnp.mean(values * values, axis=-1, keepdims=True) + EPSILON) * gain


def gated_gelu(gate_up):
    hidden_units = gate_up.shape[1] // 2
    return jax.nn.gelu(gate_up[:, :hidden_units], approximate=True) * gate_up[:, hidden_units:]


def rounded(values):
    return values.astype(jnp.bfloat16)


def distance_rows(by_distance, block):
    heads = by_distance.shape[0]
    padded = jnp.concatenate(
        [
            jnp.full((heads, block - 1), NEGATIVE, jnp.float32),
            by_distance,
            jnp.full((heads, 1), NEGATIVE, jnp.float32),
        ],
        axis=1,
    )
    pieces = padded.reshape(heads, -1, block)[:, :, ::-1]
    rows = jnp.concatenate([pieces[:, :-1], pieces[:, 1:]], axis=2)
    return jnp.concatenate([rows, jnp.full((heads, 1, 2 * block), NEGATIVE, jnp.float32)], axis=1)


def by_distance_sums(rows, block):
    heads, steps, _ = rows.shape
    zero = jnp.zeros((heads, 1, block), jnp.float32)
    pieces = jnp.concatenate([rows[:, :, :block], zero], axis=1) + jnp.concatenate(
        [zero, rows[:, :, block:]], axis=1
    )
    return pieces[:, :, ::-1].reshape(heads, -1)[:, block - 1 : block - 1 + steps * block]


def reduce_weight(grad):
    share = lax.psum_scatter(rounded(grad), ("fsdp", "ctx"), scatter_dimension=0, tiled=True)
    return lax.all_gather(share, "ctx", axis=0, tiled=True).astype(jnp.float32)


def body(tokens, encoded, cotangent, w_self, w_cross, w_ffn, gains, table, bucket_ids, block_order):
    row_count = tokens.shape[1]
    model_width = tokens.shape[2]
    head_count = table.shape[1]
    head_size = model_width // head_count
    hidden_units = w_ffn.shape[1] // 3
    block = row_count // 2
    seq_length = bucket_ids.shape[0]
    steps = seq_length // block
    ctx_place = lax.axis_index("ctx")
    table_rows = lax.all_gather(table, "fsdp", axis=0, tiled=True)
    gain_rows = lax.all_gather(gains, "fsdp", axis=1, tiled=True)
    whole_self = lax.all_gather(w_self, "fsdp", axis=0, tiled=True)
    whole_cross = lax.all_gather(w_cross, "fsdp", axis=0, tiled=True)
    whole_ffn = lax.all_gather(w_ffn, "fsdp", axis=0, tiled=True)
    gain_float = gain_rows.astype(jnp.float32)
    bucket_count = table_rows.shape[0]
    in_bucket = (
        bucket_ids[None, :] == jnp.arange(bucket_count, dtype=jnp.int32)[:, None]
    ).astype(jnp.float32)
    by_distance = lax.dot_general(
        table_rows.astype(jnp.float32),
        in_bucket,
        (((0,), (0,)), ((), ())),
        precision=lax.Precision.HIGHEST,
    )
    tiles = bias_tiles(distance_rows(by_distance, block), LANES // head_size)
    own_blocks = lax.dynamic_slice_in_dim(block_order, 2 * ctx_place, 2)
    apart = own_blocks[:, None] - block_order[None, :]
    places = jnp.where(apart < 0, steps, apart).astype(jnp.int32).reshape(-1)

    inputs = tokens[0].astype(jnp.float32)
    encoder_rows = encoded[0]
    normed_one = rounded(row_norm(inputs, gain_float[0]))
    projected = rounded(dot(normed_one, whole_self[:, : 3 * model_width]))
    queries = projected[:, :model_width]
    key_values = lax.all_gather(projected[:, model_width:], "ctx", axis=0, tiled=True)
    encoder_local = rounded(dot(encoder_rows, whole_cross[:, model_width : 3 * model_width]))
    encoder_kv = lax.all_gather(encoder_local, "ctx", axis=0, tiled=True)
    attended, weights, inverses = attention_forward(queries, key_values, head_size, tiles, places)
    after_one = inputs + dot(attended, whole_self[:, 3 * model_width :])
    normed_two = rounded(row_norm(after_one, gain_float[1]))
    cross_query = rounded(dot(normed_two, whole_cross[:, :model_width]))
    cross_rows, cross_weights, cross_inverses = attention_forward(
        cross_query, encoder_kv, head_size
    )
    after_two = after_one + dot(cross_rows, whole_cross[:, 3 * model_width :])
    normed_three = rounded(row_norm(after_two, gain_float[2]))
    gate_up = dot(normed_three, whole_ffn[:, : 2 * hidden_units])
    mixed_float, gated_back = jax.vjp(gated_gelu, gate_up)
    mixed_rows = rounded(mixed_float)
    output = rounded(after_two + dot_t(mixed_rows, whole_ffn[:, 2 * hidden_units :]))

    grad_branch_three = cotangent[0]
    grad_after_two = grad_branch_three.astype(jnp.float32)
    grad_mixed = dot(grad_branch_three, whole_ffn[:, 2 * hidden_units :])
    grad_gate_up = rounded(gated_back(grad_mixed)[0])
    grad_normed_three = dot_t(grad_gate_up, whole_ffn[:, : 2 * hidden_units])
    ffn_grad = reduce_weight(
        jnp.concatenate(
            [
                rounded(t_dot(normed_three, grad_gate_up)),
                rounded(t_dot(grad_branch_three, mixed_rows)),
            ],
            axis=1,
        )
    )
    norm_part, gain_three = jax.vjp(row_norm, after_two, gain_float[2])[1](grad_normed_three)
    grad_after_one = grad_after_two + norm_part
    grad_branch_two = rounded(grad_after_one)
    grad_cross_rows = rounded(dot_t(grad_branch_two, whole_cross[:, 3 * model_width :]))
    grad_cross_query, encoder_full = attention_backward(
        cross_query, encoder_kv, grad_cross_rows, cross_rows, cross_weights, cross_inverses,
        head_size,
    )
    encoder_own = lax.psum_scatter(encoder_full, "ctx", scatter_dimension=1, tiled=True)
    grad_normed_two = dot_t(grad_cross_query, whole_cross[:, :model_width])
    norm_part, gain_two = jax.vjp(row_norm, after_one, gain_float[1])[1](grad_normed_two)
    grad_inputs_one = grad_after_one + norm_part
    grad_branch_one = rounded(grad_inputs_one)
    grad_attended = rounded(dot_t(grad_branch_one, whole_self[:, 3 * model_width :]))
    grad_query, grad_key_full, distance_sums = attention_backward(
        queries, key_values, grad_attended, attended, weights, inverses, head_size, places, steps
    )
    grad_key_own = lax.psum_scatter(grad_key_full, "ctx", scatter_dimension=1, tiled=True)

    grad_encoder_kv = jnp.concatenate([encoder_own[0], encoder_own[1]], axis=1)
    grad_encoded = rounded(
        dot_t(grad_encoder_kv, whole_cross[:, model_width : 3 * model_width])
    )
    cross_grad = reduce_weight(
        jnp.concatenate(
            [
                rounded(t_dot(normed_two, grad_cross_query)),
                rounded(t_dot(encoder_rows, grad_encoder_kv)),
                rounded(t_dot(cross_rows, grad_branch_two)),
            ],
            axis=1,
        )
    )
    grad_table = lax.dot_general(
        in_bucket,
        by_distance_sums(distance_sums, block),
        (((1,), (1,)), ((), ())),
        precision=lax.Precision.HIGHEST,
    )
    grad_projected = jnp.concatenate([grad_query, grad_key_own[0], grad_key_own[1]], axis=1)
    grad_normed_one = dot_t(grad_projected, whole_self[:, : 3 * model_width])
    self_grad = reduce_weight(
        jnp.concatenate(
            [
                rounded(t_dot(normed_one, grad_projected)),
                rounded(t_dot(attended, grad_branch_one)),
            ],
            axis=1,
        )
    )
    norm_part, gain_one = jax.vjp(row_norm, inputs, gain_float[0])[1](grad_normed_one)
    grad_tokens = rounded(grad_inputs_one + norm_part)
    gain_terms = jnp.stack([gain_one, gain_two, gain_three])
    small = jnp.concatenate([gain_terms.reshape(-1), grad_table.reshape(-1)])
    small = lax.psum(small, ("fsdp", "ctx"))
    fsdp_place = lax.axis_index("fsdp")
    gain_total = small[: gain_terms.size].reshape(gain_terms.shape)
    table_total = small[gain_terms.size :].reshape(grad_table.shape)
    gain_own = lax.dynamic_slice_in_dim(
        gain_total, fsdp_place * gains.shape[1], gains.shape[1], axis=1
    )
    table_own = lax.dynamic_slice_in_dim(
        table_total, fsdp_place * table.shape[0], table.shape[0], axis=0
    )
    return (
        output[None],
        grad_tokens[None],
        grad_encoded[None],
        self_grad,
        cross_grad,
        ffn_grad,
        gain_own,
        table_own,
    )


def solution(mesh):
    in_specs = (
        P("fsdp", "ctx", None),
        P("fsdp", "ctx", None),
        P("fsdp", "ctx", None),
        P("fsdp", None),
        P("fsdp", None),
        P("fsdp", None),
        P(None, "fsdp"),
        P("fsdp", None),
        P(),
        P(),
    )
    out_specs = (
        P("fsdp", "ctx", None),
        P("fsdp", "ctx", None),
        P("fsdp", "ctx", None),
        P("fsdp", None),
        P("fsdp", None),
        P("fsdp", None),
        P(None, "fsdp"),
        P("fsdp", None),
    )
    return jax.shard_map(body, mesh=mesh, in_specs=in_specs, out_specs=out_specs, check_vma=False)
```

```python
import functools
import math

import jax
import jax.numpy as jnp
from jax import lax
from jax.experimental import pallas as pl
from jax.experimental.pallas import tpu as pltpu
from jax.sharding import PartitionSpec as P

NEGATIVE = -1e30
LANES = 128
VMEM_BYTES = 56 * 2**20


def dot(left, right):
    return lax.dot_general(
        left, right, (((1,), (0,)), ((), ())), preferred_element_type=jnp.float32
    )


def dot_t(left, right):
    return lax.dot_general(
        left, right, (((1,), (1,)), ((), ())), preferred_element_type=jnp.float32
    )


def t_dot(left, right):
    return lax.dot_general(
        left, right, (((0,), (0,)), ((), ())), preferred_element_type=jnp.float32
    )


def head_lanes(shape, head, head_size):
    lane = lax.broadcasted_iota(jnp.int32, shape, len(shape) - 1)
    return (lane >= head * head_size) & (lane < (head + 1) * head_size)


def only_head(values, head, head_size):
    return jnp.where(head_lanes(values.shape, head, head_size), values, jnp.zeros_like(values))


def tile_kernel(vector_ref, tile_ref):
    size = tile_ref.shape[-1]
    for head in range(vector_ref.shape[0]):
        for step in range(vector_ref.shape[1]):
            row = jnp.broadcast_to(
                vector_ref[head, step : step + 1, :], (size, 2 * size)
            )
            rolled = pltpu.roll(row, 0, 1, stride=1, stride_axis=0)
            tile_ref[head, step] = rolled[:, :size].astype(jnp.bfloat16)


def bias_tiles(vectors, group):
    head_count, steps, width = vectors.shape
    size = width // 2
    return pl.pallas_call(
        tile_kernel,
        grid=(head_count // group,),
        in_specs=[pl.BlockSpec((group, steps, width), lambda g: (g, 0, 0))],
        out_specs=pl.BlockSpec((group, steps, size, size), lambda g: (g, 0, 0, 0)),
        out_shape=jax.ShapeDtypeStruct((head_count, steps, size, size), jnp.bfloat16),
        compiler_params=pltpu.CompilerParams(vmem_limit_bytes=VMEM_BYTES),
        name="bias_tiles",
    )(vectors)


def forward_kernel(head_size, biased, *refs):
    if biased:
        place_ref, q_ref, k_ref, v_ref, tile_ref, out_ref, weight_ref, inverse_ref, score_ref = refs
    else:
        q_ref, k_ref, v_ref, out_ref, weight_ref, inverse_ref, score_ref = refs
    rows, key_total = q_ref.shape[0], k_ref.shape[0]
    group = q_ref.shape[1] // head_size
    piece = LANES
    out = jnp.zeros(q_ref.shape, jnp.float32)
    for head in range(group):
        query = only_head(q_ref[...], head, head_size)
        tops = [None] * (rows // piece)
        wide = 512
        for start in range(0, key_total, wide):
            scores = dot_t(query, k_ref[start : start + wide, :])
            for half in range(rows // piece):
                for part in range(wide // piece):
                    block = scores[
                        half * piece : (half + 1) * piece, part * piece : (part + 1) * piece
                    ]
                    key_block = start // piece + part
                    if biased:
                        place = place_ref[half * (key_total // piece) + key_block]
                        block = block + tile_ref[head, place].astype(jnp.float32)
                    score_ref[
                        half * piece : (half + 1) * piece,
                        key_block * piece : (key_block + 1) * piece,
                    ] = block
                    tops[half] = block if tops[half] is None else jnp.maximum(tops[half], block)
        top = jnp.concatenate([jnp.max(t, axis=1, keepdims=True) for t in tops], axis=0)
        total = jnp.zeros((rows, piece), jnp.float32)
        for start in range(0, key_total, piece):
            weights = jnp.exp(score_ref[:, start : start + piece] - top)
            total = total + weights
            weight_ref[head, :, start : start + piece] = weights.astype(jnp.bfloat16)
        inverse = 1.0 / jnp.sum(total, axis=1, keepdims=True)
        inverse_ref[head] = jnp.broadcast_to(inverse, (rows, LANES))
        mixed = dot(weight_ref[head], v_ref[...]) * inverse
        out = jnp.where(head_lanes(out.shape, head, head_size), mixed, out)
    out_ref[...] = out.astype(jnp.bfloat16)


def attention_forward(queries, key_values, head_size, tiles=None, places=None):
    rows, width = queries.shape
    key_total = key_values.shape[0]
    pairs = width // LANES
    group = LANES // head_size
    column = lambda shift: (lambda g, *_: (0, g + shift))
    in_specs = [
        pl.BlockSpec((rows, LANES), column(0)),
        pl.BlockSpec((key_total, LANES), column(0)),
        pl.BlockSpec((key_total, LANES), column(pairs)),
    ]
    operands = [queries, key_values, key_values]
    if tiles is not None:
        in_specs.append(
            pl.BlockSpec((group,) + tiles.shape[1:], lambda g, *_: (g, 0, 0, 0))
        )
        operands.append(tiles)
    grid_spec = pltpu.PrefetchScalarGridSpec(
        num_scalar_prefetch=0 if tiles is None else 1,
        grid=(pairs,),
        in_specs=in_specs,
        out_specs=[
            pl.BlockSpec((rows, LANES), column(0)),
            pl.BlockSpec((group, rows, key_total), lambda g, *_: (g, 0, 0)),
            pl.BlockSpec((group, rows, LANES), lambda g, *_: (g, 0, 0)),
        ],
        scratch_shapes=[pltpu.VMEM((rows, key_total), jnp.float32)],
    )
    heads = width // head_size
    return pl.pallas_call(
        functools.partial(forward_kernel, head_size, tiles is not None),
        grid_spec=grid_spec,
        out_shape=[
            jax.ShapeDtypeStruct((rows, width), jnp.bfloat16),
            jax.ShapeDtypeStruct((heads, rows, key_total), jnp.bfloat16),
            jax.ShapeDtypeStruct((heads, rows, LANES), jnp.float32),
        ],
        compiler_params=pltpu.CompilerParams(vmem_limit_bytes=VMEM_BYTES),
        cost_estimate=pl.CostEstimate(
            flops=8 * rows * key_total * width,
            bytes_accessed=2 * heads * rows * key_total + 4 * key_total * width,
            transcendentals=heads * rows * key_total,
        ),
        name="attention_forward",
    )(*(() if places is None else (places,)), *operands)


def backward_kernel(head_size, biased, *refs):
    if biased:
        (place_ref, q_ref, k_ref, v_ref, grad_ref, out_ref, weight_ref, inverse_ref,
         dq_ref, dkv_ref, dist_ref, ds_ref, sum_ref) = refs
    else:
        (q_ref, k_ref, v_ref, grad_ref, out_ref, weight_ref, inverse_ref,
         dq_ref, dkv_ref, ds_ref) = refs
    rows, key_total = q_ref.shape[0], k_ref.shape[0]
    group = q_ref.shape[1] // head_size
    piece = LANES
    wide = 512
    dq = jnp.zeros(q_ref.shape, jnp.float32)
    grads = grad_ref[...].astype(jnp.float32)
    deltas = grads * out_ref[...].astype(jnp.float32)
    if biased:
        sum_ref[...] = jnp.zeros_like(sum_ref)
    scaled_all = []
    for head in range(group):
        inverse = inverse_ref[head]
        scaled = only_head((grads * inverse).astype(jnp.bfloat16), head, head_size)
        scaled_all.append(scaled)
        delta = jnp.sum(only_head(deltas, head, head_size), axis=1, keepdims=True) * inverse
        for start in range(0, key_total, wide):
            grad_probs = dot_t(scaled, v_ref[start : start + wide, :])
            for half in range(rows // piece):
                for part in range(wide // piece):
                    lo = half * piece
                    at = start + part * piece
                    block = grad_probs[lo : lo + piece, part * piece : (part + 1) * piece]
                    weights = weight_ref[head, lo : lo + piece, at : at + piece]
                    change = weights.astype(jnp.float32) * (block - delta[lo : lo + piece])
                    ds_ref[head * rows + lo : head * rows + lo + piece, at : at + piece] = (
                        change.astype(jnp.bfloat16)
                    )
                    if biased:
                        place = place_ref[half * (key_total // piece) + at // piece]
                        sum_ref[head, place] += change
        mixed = dot(ds_ref[head * rows : (head + 1) * rows, :], k_ref[...])
        dq = jnp.where(head_lanes(dq.shape, head, head_size), mixed, dq)
    dq_ref[...] = dq.astype(jnp.bfloat16)
    queries = jnp.concatenate(
        [only_head(q_ref[...], head, head_size) for head in range(group)], axis=0
    )
    scaled_rows = jnp.concatenate(scaled_all, axis=0)
    for start in range(0, key_total, wide):
        dkv_ref[0, start : start + wide, :] = t_dot(
            ds_ref[:, start : start + wide], queries
        ).astype(jnp.bfloat16)
        weights = jnp.concatenate(
            [weight_ref[head, :, start : start + wide] for head in range(group)], axis=0
        )
        dkv_ref[1, start : start + wide, :] = t_dot(weights, scaled_rows).astype(
            jnp.bfloat16
        )
    if biased:
        steps = dist_ref.shape[1]
        down = lax.broadcasted_iota(jnp.int32, (piece, piece), 0)
        across = lax.broadcasted_iota(jnp.int32, (piece, piece), 1)
        flip = (down + across == piece - 1).astype(jnp.bfloat16)

        def fold(step, carry):
            for head in range(group):
                block = sum_ref[head, step]
                high = block.astype(jnp.bfloat16)
                low = (block - high.astype(jnp.float32)).astype(jnp.bfloat16)
                turned = dot(flip, high) + dot(flip, low)
                padded = jnp.concatenate([turned, jnp.zeros_like(turned)], axis=1)
                rolled = pltpu.roll(padded, piece + 1, 1, stride=1, stride_axis=0)
                dist_ref[head, pl.ds(step, 1), :] = jnp.sum(rolled, axis=0, keepdims=True)
            return carry

        lax.fori_loop(0, steps, fold, 0)


def attention_backward(
    queries, key_values, grads, outs, weights, inverses, head_size, places=None, steps=0
):
    rows, width = queries.shape
    key_total = key_values.shape[0]
    pairs = width // LANES
    group = LANES // head_size
    heads = width // head_size
    biased = places is not None
    column = lambda shift: (lambda g, *_: (0, g + shift))
    row_block = pl.BlockSpec((rows, LANES), column(0))
    key_block = pl.BlockSpec((key_total, LANES), column(0))
    out_specs = [row_block, pl.BlockSpec((2, key_total, LANES), lambda g, *_: (0, 0, g))]
    out_shape = [
        jax.ShapeDtypeStruct((rows, width), jnp.bfloat16),
        jax.ShapeDtypeStruct((2, key_total, width), jnp.bfloat16),
    ]
    scratch = [pltpu.VMEM((group * rows, key_total), jnp.bfloat16)]
    if biased:
        out_specs.append(pl.BlockSpec((group, steps, 2 * LANES), lambda g, *_: (g, 0, 0)))
        out_shape.append(jax.ShapeDtypeStruct((heads, steps, 2 * LANES), jnp.float32))
        scratch.append(pltpu.VMEM((group, steps + 1, LANES, LANES), jnp.float32))
    grid_spec = pltpu.PrefetchScalarGridSpec(
        num_scalar_prefetch=1 if biased else 0,
        grid=(pairs,),
        in_specs=[
            row_block,
            key_block,
            pl.BlockSpec((key_total, LANES), column(pairs)),
            row_block,
            row_block,
            pl.BlockSpec((group, rows, key_total), lambda g, *_: (g, 0, 0)),
            pl.BlockSpec((group, rows, LANES), lambda g, *_: (g, 0, 0)),
        ],
        out_specs=out_specs,
        scratch_shapes=scratch,
    )
    return pl.pallas_call(
        functools.partial(backward_kernel, head_size, biased),
        grid_spec=grid_spec,
        out_shape=out_shape,
        compiler_params=pltpu.CompilerParams(vmem_limit_bytes=VMEM_BYTES),
        cost_estimate=pl.CostEstimate(
            flops=16 * rows * key_total * width,
            bytes_accessed=2 * heads * rows * key_total + 8 * key_total * width,
            transcendentals=0,
        ),
        name="attention_backward",
    )(
        *((places,) if biased else ()),
        queries, key_values, key_values, grads, outs, weights, inverses,
    )


EPSILON = 1e-06


def row_norm(values, gain):
    return values * lax.rsqrt(jnp.mean(values * values, axis=-1, keepdims=True) + EPSILON) * gain


def gated_gelu(gate_up):
    hidden_units = gate_up.shape[1] // 2
    return jax.nn.gelu(gate_up[:, :hidden_units], approximate=True) * gate_up[:, hidden_units:]


def rounded(values):
    return values.astype(jnp.bfloat16)


def distance_rows(by_distance, block):
    heads = by_distance.shape[0]
    padded = jnp.concatenate(
        [
            jnp.full((heads, block - 1), NEGATIVE, jnp.float32),
            by_distance,
            jnp.full((heads, 1), NEGATIVE, jnp.float32),
        ],
        axis=1,
    )
    pieces = padded.reshape(heads, -1, block)[:, :, ::-1]
    rows = jnp.concatenate([pieces[:, :-1], pieces[:, 1:]], axis=2)
    return jnp.concatenate([rows, jnp.full((heads, 1, 2 * block), NEGATIVE, jnp.float32)], axis=1)


def by_distance_sums(rows, block):
    heads, steps, _ = rows.shape
    zero = jnp.zeros((heads, 1, block), jnp.float32)
    pieces = jnp.concatenate([rows[:, :, :block], zero], axis=1) + jnp.concatenate(
        [zero, rows[:, :, block:]], axis=1
    )
    return pieces[:, :, ::-1].reshape(heads, -1)[:, block - 1 : block - 1 + steps * block]


def bit_count(axis_name):
    return int(math.log2(lax.axis_size(axis_name)))


def swap(values, axis_name, bit):
    size = lax.axis_size(axis_name)
    return lax.ppermute(values, axis_name, [(i, i ^ (1 << bit)) for i in range(size)])


def own_bit(axis_name, bit):
    return (lax.axis_index(axis_name) >> bit) & 1


def pick(values, index, axis):
    return lax.dynamic_index_in_dim(values, index, axis, keepdims=False)


def gather_rows(share):
    rows = share.shape[0]
    place = lax.axis_index("fsdp")
    whole = jnp.zeros((rows * lax.axis_size("fsdp"),) + share.shape[1:], share.dtype)
    held = [(share, place)]
    for bit in reversed(range(bit_count("fsdp"))):
        held = held + [(swap(piece, "fsdp", bit), at ^ (1 << bit)) for piece, at in held]
    for piece, at in held:
        whole = lax.dynamic_update_slice_in_dim(whole, piece, at * rows, 0)
    return whole


class Product:
    def __init__(self, left, right, parts):
        bits = int(math.log2(parts))
        self.left = left.reshape((left.shape[0],) + (2,) * bits + (left.shape[1] // parts,))
        self.right = right

    def take(self, bit):
        part = Product.__new__(Product)
        part.left = pick(self.left, bit, self.left.ndim - 2)
        part.right = self.right
        return part

    def value(self):
        return t_dot(self.left, self.right)


class Ready:
    def __init__(self, values, parts):
        bits = int(math.log2(parts))
        self.values = values.reshape(
            (2,) * bits + (values.shape[0] // parts, values.shape[1])
        )

    def take(self, bit):
        part = Ready.__new__(Ready)
        part.values = pick(self.values, bit, self.values.ndim - 3)
        return part

    def value(self):
        return self.values


def reduce_rows(terms):
    received = []
    for bit in range(bit_count("fsdp")):
        mine = own_bit("fsdp", bit)
        send = jnp.concatenate([term.take(1 - mine).value() for term in terms], axis=-1)
        for item in received:
            send = send + pick(item, 1 - mine, item.ndim - 3).astype(jnp.float32)
        terms = [term.take(mine) for term in terms]
        received = [pick(item, mine, item.ndim - 3) for item in received]
        received.append(swap(rounded(send), "fsdp", bit))
    total = jnp.concatenate([term.value() for term in terms], axis=-1)
    for item in received:
        total = total + item.astype(jnp.float32)
    total = rounded(total)
    for bit in range(bit_count("ctx")):
        mine = own_bit("ctx", bit)
        halves = total.reshape(2, total.shape[0] // 2, total.shape[1])
        other = swap(pick(halves, 1 - mine, 0), "ctx", bit)
        total = rounded(pick(halves, mine, 0).astype(jnp.float32) + other.astype(jnp.float32))
    for bit in reversed(range(bit_count("ctx"))):
        mine = own_bit("ctx", bit)
        other = swap(total, "ctx", bit)
        total = jnp.where(
            mine == 0,
            jnp.concatenate([total, other], axis=0),
            jnp.concatenate([other, total], axis=0),
        )
    return total


def body(tokens, encoded, cotangent, w_self, w_cross, w_ffn, gains, table, bucket_ids, block_order):
    row_count = tokens.shape[1]
    model_width = tokens.shape[2]
    head_count = table.shape[1]
    head_size = model_width // head_count
    hidden_units = w_ffn.shape[1] // 3
    block = row_count // 2
    seq_length = bucket_ids.shape[0]
    steps = seq_length // block
    ctx_place = lax.axis_index("ctx")
    fsdp_size = lax.axis_size("fsdp")
    small = lax.all_gather(
        jnp.concatenate([gains.reshape(1, -1), table.reshape(1, -1)], axis=1),
        "fsdp", axis=0, tiled=True,
    )
    gain_rows = jnp.transpose(
        small[:, : gains.size].reshape((fsdp_size,) + gains.shape), (1, 0, 2)
    ).reshape(gains.shape[0], -1)
    table_rows = small[:, gains.size :].reshape(-1, head_count)
    whole_self = gather_rows(w_self)
    whole_cross = gather_rows(w_cross)
    whole_ffn = gather_rows(w_ffn)
    gain_float = gain_rows.astype(jnp.float32)
    bucket_count = table_rows.shape[0]
    in_bucket = (
        bucket_ids[None, :] == jnp.arange(bucket_count, dtype=jnp.int32)[:, None]
    ).astype(jnp.float32)
    by_distance = lax.dot_general(
        table_rows.astype(jnp.float32),
        in_bucket,
        (((0,), (0,)), ((), ())),
        precision=lax.Precision.HIGHEST,
    )
    tiles = bias_tiles(distance_rows(by_distance, block), LANES // head_size)
    own_blocks = lax.dynamic_slice_in_dim(block_order, 2 * ctx_place, 2)
    apart = own_blocks[:, None] - block_order[None, :]
    places = jnp.where(apart < 0, steps, apart).astype(jnp.int32).reshape(-1)

    inputs = tokens[0].astype(jnp.float32)
    encoder_rows = encoded[0]
    normed_one = rounded(row_norm(inputs, gain_float[0]))
    projected = rounded(dot(normed_one, whole_self[:, : 3 * model_width]))
    queries = projected[:, :model_width]
    key_values = lax.all_gather(projected[:, model_width:], "ctx", axis=0, tiled=True)
    encoder_local = rounded(dot(encoder_rows, whole_cross[:, model_width : 3 * model_width]))
    encoder_kv = lax.all_gather(encoder_local, "ctx", axis=0, tiled=True)
    attended, weights, inverses = attention_forward(queries, key_values, head_size, tiles, places)
    after_one = inputs + dot(attended, whole_self[:, 3 * model_width :])
    normed_two = rounded(row_norm(after_one, gain_float[1]))
    cross_query = rounded(dot(normed_two, whole_cross[:, :model_width]))
    cross_rows, cross_weights, cross_inverses = attention_forward(
        cross_query, encoder_kv, head_size
    )
    after_two = after_one + dot(cross_rows, whole_cross[:, 3 * model_width :])
    normed_three = rounded(row_norm(after_two, gain_float[2]))
    gate_up = dot(normed_three, whole_ffn[:, : 2 * hidden_units])
    mixed_float, gated_back = jax.vjp(gated_gelu, gate_up)
    mixed_rows = rounded(mixed_float)
    output = rounded(after_two + dot_t(mixed_rows, whole_ffn[:, 2 * hidden_units :]))

    grad_branch_three = cotangent[0]
    grad_after_two = grad_branch_three.astype(jnp.float32)
    grad_mixed = dot(grad_branch_three, whole_ffn[:, 2 * hidden_units :])
    grad_gate_up = rounded(gated_back(grad_mixed)[0])
    grad_normed_three = dot_t(grad_gate_up, whole_ffn[:, : 2 * hidden_units])
    ffn_grad = reduce_rows(
        [
            Product(normed_three, grad_gate_up, fsdp_size),
            Product(grad_branch_three, mixed_rows, fsdp_size),
        ]
    )
    norm_part, gain_three = jax.vjp(row_norm, after_two, gain_float[2])[1](grad_normed_three)
    grad_after_one = grad_after_two + norm_part
    grad_branch_two = rounded(grad_after_one)
    grad_cross_rows = rounded(dot_t(grad_branch_two, whole_cross[:, 3 * model_width :]))
    grad_cross_query, encoder_full = attention_backward(
        cross_query, encoder_kv, grad_cross_rows, cross_rows, cross_weights, cross_inverses,
        head_size,
    )
    encoder_own = lax.psum_scatter(encoder_full, "ctx", scatter_dimension=1, tiled=True)
    cross_grad = reduce_rows(
        [
            Product(normed_two, grad_cross_query, fsdp_size),
            Product(cross_rows, grad_branch_two, fsdp_size),
        ]
    )
    grad_normed_two = dot_t(grad_cross_query, whole_cross[:, :model_width])
    norm_part, gain_two = jax.vjp(row_norm, after_one, gain_float[1])[1](grad_normed_two)
    grad_inputs_one = grad_after_one + norm_part
    grad_branch_one = rounded(grad_inputs_one)
    grad_attended = rounded(dot_t(grad_branch_one, whole_self[:, 3 * model_width :]))
    grad_query, grad_key_full, distance_sums = attention_backward(
        queries, key_values, grad_attended, attended, weights, inverses, head_size, places, steps
    )
    grad_key_own = lax.psum_scatter(grad_key_full, "ctx", scatter_dimension=1, tiled=True)

    grad_encoder_kv = jnp.concatenate([encoder_own[0], encoder_own[1]], axis=1)
    grad_encoded = rounded(
        dot_t(grad_encoder_kv, whole_cross[:, model_width : 3 * model_width])
    )
    encoder_grad = reduce_rows([Product(encoder_rows, grad_encoder_kv, fsdp_size)])
    grad_table = lax.dot_general(
        in_bucket,
        by_distance_sums(distance_sums, block),
        (((1,), (1,)), ((), ())),
        precision=lax.Precision.HIGHEST,
    )
    query_grad = reduce_rows(
        [
            Product(normed_one, grad_query, fsdp_size),
            Product(attended, grad_branch_one, fsdp_size),
        ]
    )
    grad_projected = jnp.concatenate([grad_query, grad_key_own[0], grad_key_own[1]], axis=1)
    grad_normed_one = dot_t(grad_projected, whole_self[:, : 3 * model_width])
    norm_part, gain_one = jax.vjp(row_norm, inputs, gain_float[0])[1](grad_normed_one)
    grad_tokens = rounded(grad_inputs_one + norm_part)
    gain_columns = jnp.stack([gain_one, gain_two, gain_three], axis=1)
    table_columns = jnp.pad(
        grad_table.reshape(fsdp_size, -1, head_count),
        ((0, 0), (0, gains.shape[1] - table.shape[0]), (0, 0)),
    ).reshape(model_width, head_count)
    small_columns = jnp.pad(
        jnp.concatenate([gain_columns, table_columns], axis=1),
        ((0, 0), (0, LANES - gains.shape[0] - head_count)),
    )
    key_grad = reduce_rows(
        [
            Product(normed_one, grad_projected[:, model_width:], fsdp_size),
            Ready(small_columns, fsdp_size),
        ]
    )
    wide = lambda values: values.astype(jnp.float32)
    self_grad = wide(
        jnp.concatenate(
            [
                query_grad[:, :model_width],
                key_grad[:, : 2 * model_width],
                query_grad[:, model_width:],
            ],
            axis=1,
        )
    )
    cross_grad = wide(
        jnp.concatenate(
            [cross_grad[:, :model_width], encoder_grad, cross_grad[:, model_width:]], axis=1
        )
    )
    ffn_grad = wide(ffn_grad)
    small_own = wide(key_grad[:, 2 * model_width :])
    gain_own = jnp.transpose(small_own[:, : gains.shape[0]])
    table_own = small_own[: table.shape[0], gains.shape[0] : gains.shape[0] + head_count]
    return (
        output[None],
        grad_tokens[None],
        grad_encoded[None],
        self_grad,
        cross_grad,
        ffn_grad,
        gain_own,
        table_own,
    )


def solution(mesh):
    in_specs = (
        P("fsdp", "ctx", None),
        P("fsdp", "ctx", None),
        P("fsdp", "ctx", None),
        P("fsdp", None),
        P("fsdp", None),
        P("fsdp", None),
        P(None, "fsdp"),
        P("fsdp", None),
        P(),
        P(),
    )
    out_specs = (
        P("fsdp", "ctx", None),
        P("fsdp", "ctx", None),
        P("fsdp", "ctx", None),
        P("fsdp", None),
        P("fsdp", None),
        P("fsdp", None),
        P(None, "fsdp"),
        P("fsdp", None),
    )
    return jax.shard_map(body, mesh=mesh, in_specs=in_specs, out_specs=out_specs, check_vma=False)
```

```python
import functools
import math

import jax
import jax.numpy as jnp
from jax import lax
from jax.experimental import pallas as pl
from jax.experimental.pallas import tpu as pltpu
from jax.sharding import PartitionSpec as P

NEGATIVE = -1e30
LANES = 128
VMEM_BYTES = 56 * 2**20


def dot(left, right):
    return lax.dot_general(
        left, right, (((1,), (0,)), ((), ())), preferred_element_type=jnp.float32
    )


def dot_t(left, right):
    return lax.dot_general(
        left, right, (((1,), (1,)), ((), ())), preferred_element_type=jnp.float32
    )


def t_dot(left, right):
    return lax.dot_general(
        left, right, (((0,), (0,)), ((), ())), preferred_element_type=jnp.float32
    )


def head_lanes(shape, head, head_size):
    lane = lax.broadcasted_iota(jnp.int32, shape, len(shape) - 1)
    return (lane >= head * head_size) & (lane < (head + 1) * head_size)


def only_head(values, head, head_size):
    return jnp.where(head_lanes(values.shape, head, head_size), values, jnp.zeros_like(values))


def tile_kernel(vector_ref, tile_ref):
    size = tile_ref.shape[-1]
    for head in range(vector_ref.shape[0]):
        for step in range(vector_ref.shape[1]):
            row = jnp.broadcast_to(
                vector_ref[head, step : step + 1, :], (size, 2 * size)
            )
            rolled = pltpu.roll(row, 0, 1, stride=1, stride_axis=0)
            tile_ref[head, step] = rolled[:, :size].astype(jnp.bfloat16)


def bias_tiles(vectors, group):
    head_count, steps, width = vectors.shape
    size = width // 2
    return pl.pallas_call(
        tile_kernel,
        grid=(head_count // group,),
        in_specs=[pl.BlockSpec((group, steps, width), lambda g: (g, 0, 0))],
        out_specs=pl.BlockSpec((group, steps, size, size), lambda g: (g, 0, 0, 0)),
        out_shape=jax.ShapeDtypeStruct((head_count, steps, size, size), jnp.bfloat16),
        compiler_params=pltpu.CompilerParams(vmem_limit_bytes=VMEM_BYTES),
        name="bias_tiles",
    )(vectors)


def forward_kernel(head_size, biased, *refs):
    if biased:
        place_ref, q_ref, k_ref, v_ref, tile_ref, out_ref, weight_ref, inverse_ref, score_ref = refs
    else:
        q_ref, k_ref, v_ref, out_ref, weight_ref, inverse_ref, score_ref = refs
    rows, key_total = q_ref.shape[0], k_ref.shape[0]
    group = q_ref.shape[1] // head_size
    piece = LANES
    out = jnp.zeros(q_ref.shape, jnp.float32)
    for head in range(group):
        query = only_head(q_ref[...], head, head_size)
        tops = [None] * (rows // piece)
        wide = 512
        for start in range(0, key_total, wide):
            scores = dot_t(query, k_ref[start : start + wide, :])
            for half in range(rows // piece):
                for part in range(wide // piece):
                    block = scores[
                        half * piece : (half + 1) * piece, part * piece : (part + 1) * piece
                    ]
                    key_block = start // piece + part
                    if biased:
                        place = place_ref[half * (key_total // piece) + key_block]
                        block = block + tile_ref[head, place].astype(jnp.float32)
                    score_ref[
                        half * piece : (half + 1) * piece,
                        key_block * piece : (key_block + 1) * piece,
                    ] = block
                    tops[half] = block if tops[half] is None else jnp.maximum(tops[half], block)
        top = jnp.concatenate([jnp.max(t, axis=1, keepdims=True) for t in tops], axis=0)
        total = jnp.zeros((rows, piece), jnp.float32)
        for start in range(0, key_total, piece):
            weights = jnp.exp(score_ref[:, start : start + piece] - top)
            total = total + weights
            weight_ref[head, :, start : start + piece] = weights.astype(jnp.bfloat16)
        inverse = 1.0 / jnp.sum(total, axis=1, keepdims=True)
        inverse_ref[head] = jnp.broadcast_to(inverse, (rows, LANES))
        mixed = dot(weight_ref[head], v_ref[...]) * inverse
        out = jnp.where(head_lanes(out.shape, head, head_size), mixed, out)
    out_ref[...] = out.astype(jnp.bfloat16)


def attention_forward(queries, key_values, head_size, tiles=None, places=None):
    rows, width = queries.shape
    key_total = key_values.shape[0]
    pairs = width // LANES
    group = LANES // head_size
    column = lambda shift: (lambda g, *_: (0, g + shift))
    in_specs = [
        pl.BlockSpec((rows, LANES), column(0)),
        pl.BlockSpec((key_total, LANES), column(0)),
        pl.BlockSpec((key_total, LANES), column(pairs)),
    ]
    operands = [queries, key_values, key_values]
    if tiles is not None:
        in_specs.append(
            pl.BlockSpec((group,) + tiles.shape[1:], lambda g, *_: (g, 0, 0, 0))
        )
        operands.append(tiles)
    grid_spec = pltpu.PrefetchScalarGridSpec(
        num_scalar_prefetch=0 if tiles is None else 1,
        grid=(pairs,),
        in_specs=in_specs,
        out_specs=[
            pl.BlockSpec((rows, LANES), column(0)),
            pl.BlockSpec((group, rows, key_total), lambda g, *_: (g, 0, 0)),
            pl.BlockSpec((group, rows, LANES), lambda g, *_: (g, 0, 0)),
        ],
        scratch_shapes=[pltpu.VMEM((rows, key_total), jnp.float32)],
    )
    heads = width // head_size
    return pl.pallas_call(
        functools.partial(forward_kernel, head_size, tiles is not None),
        grid_spec=grid_spec,
        out_shape=[
            jax.ShapeDtypeStruct((rows, width), jnp.bfloat16),
            jax.ShapeDtypeStruct((heads, rows, key_total), jnp.bfloat16),
            jax.ShapeDtypeStruct((heads, rows, LANES), jnp.float32),
        ],
        compiler_params=pltpu.CompilerParams(vmem_limit_bytes=VMEM_BYTES),
        cost_estimate=pl.CostEstimate(flops=1, bytes_accessed=1, transcendentals=0),
        name="attention_forward",
    )(*(() if places is None else (places,)), *operands)


def backward_kernel(head_size, biased, *refs):
    if biased:
        (q_ref, k_ref, v_ref, grad_ref, out_ref, weight_ref, inverse_ref,
         dq_ref, dkv_ref, dist_ref, ds_ref) = refs
    else:
        (q_ref, k_ref, v_ref, grad_ref, out_ref, weight_ref, inverse_ref,
         dq_ref, dkv_ref, ds_ref) = refs
    rows, key_total = q_ref.shape[0], k_ref.shape[0]
    group = q_ref.shape[1] // head_size
    piece = LANES
    wide = 512
    dq = jnp.zeros(q_ref.shape, jnp.float32)
    grads = grad_ref[...].astype(jnp.float32)
    deltas = grads * out_ref[...].astype(jnp.float32)
    scaled_all = []
    for head in range(group):
        inverse = inverse_ref[head]
        scaled = only_head((grads * inverse).astype(jnp.bfloat16), head, head_size)
        scaled_all.append(scaled)
        delta = jnp.sum(only_head(deltas, head, head_size), axis=1, keepdims=True) * inverse
        for start in range(0, key_total, wide):
            grad_probs = dot_t(scaled, v_ref[start : start + wide, :])
            for half in range(rows // piece):
                for part in range(wide // piece):
                    lo = half * piece
                    at = start + part * piece
                    block = grad_probs[lo : lo + piece, part * piece : (part + 1) * piece]
                    weights = weight_ref[head, lo : lo + piece, at : at + piece]
                    change = weights.astype(jnp.float32) * (block - delta[lo : lo + piece])
                    ds_ref[head * rows + lo : head * rows + lo + piece, at : at + piece] = (
                        change.astype(jnp.bfloat16)
                    )
        mixed = dot(ds_ref[head * rows : (head + 1) * rows, :], k_ref[...])
        dq = jnp.where(head_lanes(dq.shape, head, head_size), mixed, dq)
    dq_ref[...] = dq.astype(jnp.bfloat16)
    queries = jnp.concatenate(
        [only_head(q_ref[...], head, head_size) for head in range(group)], axis=0
    )
    scaled_rows = jnp.concatenate(scaled_all, axis=0)
    for start in range(0, key_total, wide):
        dkv_ref[0, start : start + wide, :] = t_dot(
            ds_ref[:, start : start + wide], queries
        ).astype(jnp.bfloat16)
        weights = jnp.concatenate(
            [weight_ref[head, :, start : start + wide] for head in range(group)], axis=0
        )
        dkv_ref[1, start : start + wide, :] = t_dot(weights, scaled_rows).astype(
            jnp.bfloat16
        )
    if biased:
        down = lax.broadcasted_iota(jnp.int32, (piece, piece), 0)
        across = lax.broadcasted_iota(jnp.int32, (piece, piece), 1)
        flip = (down + across == piece - 1).astype(jnp.bfloat16)
        for head in range(group):
            for half in range(rows // piece):
                lo = head * rows + half * piece
                for start in range(0, key_total, wide):
                    turned = dot(flip, ds_ref[lo : lo + piece, start : start + wide])
                    for part in range(wide // piece):
                        block = turned[:, part * piece : (part + 1) * piece]
                        rolled = pltpu.roll(block, 1, 1, stride=1, stride_axis=0)
                        later = jnp.sum(
                            jnp.where(across <= down, rolled, 0.0), axis=0, keepdims=True
                        )
                        every = jnp.sum(rolled, axis=0, keepdims=True)
                        at = half * (key_total // piece) + start // piece + part
                        dist_ref[head, at : at + 1, :piece] = later
                        dist_ref[head, at : at + 1, piece:] = every - later


def attention_backward(
    queries, key_values, grads, outs, weights, inverses, head_size, biased, first=0, count=None
):
    rows, width = queries.shape
    key_total = key_values.shape[0]
    pairs = width // LANES
    count = pairs if count is None else count
    group = LANES // head_size
    column = lambda shift: (lambda g: (0, g + shift))
    head_block = lambda g: (g + first, 0, 0)
    row_block = pl.BlockSpec((rows, LANES), column(first))
    blocks = rows // LANES * (key_total // LANES)
    out_specs = [
        pl.BlockSpec((rows, LANES), column(0)),
        pl.BlockSpec((2, key_total, LANES), lambda g: (0, 0, g)),
    ]
    out_shape = [
        jax.ShapeDtypeStruct((rows, count * LANES), jnp.bfloat16),
        jax.ShapeDtypeStruct((2, key_total, count * LANES), jnp.bfloat16),
    ]
    if biased:
        out_specs.append(pl.BlockSpec((group, blocks, 2 * LANES), lambda g: (g, 0, 0)))
        out_shape.append(
            jax.ShapeDtypeStruct((group * count, blocks, 2 * LANES), jnp.float32)
        )
    return pl.pallas_call(
        functools.partial(backward_kernel, head_size, biased),
        grid=(count,),
        in_specs=[
            row_block,
            pl.BlockSpec((key_total, LANES), column(first)),
            pl.BlockSpec((key_total, LANES), column(first + pairs)),
            row_block,
            row_block,
            pl.BlockSpec((group, rows, key_total), head_block),
            pl.BlockSpec((group, rows, LANES), head_block),
        ],
        out_specs=out_specs,
        out_shape=out_shape,
        scratch_shapes=[pltpu.VMEM((group * rows, key_total), jnp.bfloat16)],
        compiler_params=pltpu.CompilerParams(vmem_limit_bytes=VMEM_BYTES),
        cost_estimate=pl.CostEstimate(flops=1, bytes_accessed=1, transcendentals=0),
        name="attention_backward",
    )(queries, key_values, key_values, grads, outs, weights, inverses)


def place_kernel(count, at_ref, *refs):
    pieces, whole_ref, held_ref, in_sems, out_sems = refs[:count], *refs[count:]
    rows = held_ref.shape[1]
    parts = in_sems.shape[1]
    width = held_ref.shape[2] // parts
    loads, stores = [], []
    for index in range(count):
        start = pl.multiple_of(at_ref[index] * rows, rows)
        for part in range(parts):
            columns = pl.ds(part * width, width)
            held = held_ref.at[index, :, columns]
            loads.append(
                pltpu.make_async_copy(
                    pieces[index].at[:, columns], held, in_sems.at[index, part]
                )
            )
            stores.append(
                pltpu.make_async_copy(
                    held, whole_ref.at[pl.ds(start, rows), columns], out_sems.at[index, part]
                )
            )
    for load in loads:
        load.start()
    for load, store in zip(loads, stores):
        load.wait()
        store.start()
    for store in stores:
        store.wait()


def place_rows(pieces, places):
    rows, width = pieces[0].shape
    count = len(pieces)
    parts = width // 1024
    return pl.pallas_call(
        functools.partial(place_kernel, count),
        grid_spec=pltpu.PrefetchScalarGridSpec(
            num_scalar_prefetch=1,
            grid=(1,),
            in_specs=[pl.BlockSpec(memory_space=pl.ANY)] * count,
            out_specs=pl.BlockSpec(memory_space=pl.ANY),
            scratch_shapes=[
                pltpu.VMEM((count, rows, width), pieces[0].dtype),
                pltpu.SemaphoreType.DMA((count, parts)),
                pltpu.SemaphoreType.DMA((count, parts)),
            ],
        ),
        out_shape=jax.ShapeDtypeStruct((rows * count, width), pieces[0].dtype),
        compiler_params=pltpu.CompilerParams(vmem_limit_bytes=VMEM_BYTES),
        name="place_rows",
    )(jnp.stack(places).astype(jnp.int32), *pieces)


EPSILON = 1e-06


def row_norm(values, gain):
    return values * lax.rsqrt(jnp.mean(values * values, axis=-1, keepdims=True) + EPSILON) * gain


def gated_gelu(gate_up):
    hidden_units = gate_up.shape[1] // 2
    return jax.nn.gelu(gate_up[:, :hidden_units], approximate=True) * gate_up[:, hidden_units:]


def rounded(values):
    return values.astype(jnp.bfloat16)


def distance_rows(by_distance, block):
    heads = by_distance.shape[0]
    padded = jnp.concatenate(
        [
            jnp.full((heads, block - 1), NEGATIVE, jnp.float32),
            by_distance,
            jnp.full((heads, 1), NEGATIVE, jnp.float32),
        ],
        axis=1,
    )
    pieces = padded.reshape(heads, -1, block)[:, :, ::-1]
    rows = jnp.concatenate([pieces[:, :-1], pieces[:, 1:]], axis=2)
    return jnp.concatenate([rows, jnp.full((heads, 1, 2 * block), NEGATIVE, jnp.float32)], axis=1)


def by_distance_sums(rows, block):
    heads, steps, _ = rows.shape
    zero = jnp.zeros((heads, 1, block), jnp.float32)
    pieces = jnp.concatenate([rows[:, :, :block], zero], axis=1) + jnp.concatenate(
        [zero, rows[:, :, block:]], axis=1
    )
    return pieces[:, :, ::-1].reshape(heads, -1)[:, block - 1 : block - 1 + steps * block]


def bit_count(axis_name):
    return int(math.log2(lax.axis_size(axis_name)))


def swap(values, axis_name, bit):
    size = lax.axis_size(axis_name)
    return lax.ppermute(values, axis_name, [(i, i ^ (1 << bit)) for i in range(size)])


def own_bit(axis_name, bit):
    return (lax.axis_index(axis_name) >> bit) & 1


def pick(values, index, axis):
    return lax.dynamic_index_in_dim(values, index, axis, keepdims=False)


def after(value, *others):
    return lax.optimization_barrier((value,) + others)[0]


def far_rows(share):
    held = [(share, lax.axis_index("fsdp"))]
    for bit in reversed(range(1, bit_count("fsdp"))):
        held = held + [(swap(piece, "fsdp", bit), at ^ (1 << bit)) for piece, at in held]
    return held


def near_rows(held):
    return held + [(swap(piece, "fsdp", 0), at ^ 1) for piece, at in held]


def whole_rows(held):
    held = near_rows(held)
    return place_rows([piece for piece, _ in held], [at for _, at in held])


class Product:
    def __init__(self, left, right, parts):
        bits = int(math.log2(parts))
        self.left = left.reshape((left.shape[0],) + (2,) * bits + (left.shape[1] // parts,))
        self.right = right

    def take(self, bit):
        part = Product.__new__(Product)
        part.left = pick(self.left, bit, self.left.ndim - 2)
        part.right = self.right
        return part

    def value(self):
        return t_dot(self.left, self.right)


class Ready:
    def __init__(self, values, parts):
        bits = int(math.log2(parts))
        self.values = values.reshape(
            (2,) * bits + (values.shape[0] // parts, values.shape[1])
        )

    def take(self, bit):
        part = Ready.__new__(Ready)
        part.values = pick(self.values, bit, self.values.ndim - 3)
        return part

    def value(self):
        return self.values


def joined(own, other, mine):
    return jnp.where(
        mine == 0, jnp.stack([own, other], axis=-3), jnp.stack([other, own], axis=-3)
    )


class Reduction:
    def __init__(self, terms, *stages):
        self.terms = terms
        self.received = []
        self.kept = None
        self.pending = None
        self.gathered = None
        self.plan = []
        for stage in stages:
            bits = [(stage, bit) for bit in range(bit_count("fsdp" if stage == "fsdp" else "ctx"))]
            self.plan += reversed(bits) if stage == "gather" else bits

    def shard(self):
        total = jnp.concatenate([term.value() for term in self.terms], axis=-1)
        for item in self.received:
            total = total + item.astype(jnp.float32)
        return rounded(total)

    def merged(self):
        if self.gathered is not None:
            own, bit = self.gathered
            return joined(own, self.pending, own_bit("ctx", bit))
        if self.kept is not None:
            return rounded(self.kept.astype(jnp.float32) + self.pending.astype(jnp.float32))
        total = self.shard()
        parts = lax.axis_size("ctx")
        return total.reshape(
            (2,) * bit_count("ctx") + (total.shape[0] // parts, total.shape[1])
        )

    def settle(self, main):
        main = tuple(main)
        if self.pending is not None:
            self.pending, *main = lax.optimization_barrier((self.pending,) + main)
        elif self.received:
            *self.received, last = lax.optimization_barrier(tuple(self.received) + (main,))
            main = last
        return tuple(main)

    def prepare(self):
        kind, bit = self.step = self.plan.pop(0)
        if kind == "gather":
            total = self.merged()
            self.gathered = (total, bit)
            return total
        mine = own_bit(kind, bit)
        if kind == "ctx":
            total = self.merged()
            self.kept = pick(total, mine, total.ndim - 3)
            return pick(total, 1 - mine, total.ndim - 3)
        send = jnp.concatenate([term.take(1 - mine).value() for term in self.terms], axis=-1)
        for item in self.received:
            send = send + pick(item, 1 - mine, item.ndim - 3).astype(jnp.float32)
        self.terms = [term.take(mine) for term in self.terms]
        self.received = [pick(item, mine, item.ndim - 3) for item in self.received]
        return rounded(send)

    def exchange(self, send):
        kind, bit = self.step
        other = swap(send, "fsdp" if kind == "fsdp" else "ctx", bit)
        if kind == "fsdp":
            self.received.append(other)
        else:
            self.pending = other

    def result(self):
        total = self.merged()
        return total.reshape(-1, total.shape[-1])


def finish(item):
    while item.plan:
        advance([item])
    return item.shard()


def advance(sums, *main):
    if main:
        for item in sums:
            main = item.settle(main)
    sends = [item.prepare() for item in sums]
    held = lax.optimization_barrier(tuple(sends) + tuple(main))
    for item, send in zip(sums, held):
        item.exchange(send)
    main = held[len(sums) :]
    return main[0] if len(main) == 1 else main


def weighed(weight, grad):
    return jnp.sum(weight.astype(jnp.float32) * grad[:, : weight.shape[1]], axis=1)


def body(tokens, encoded, cotangent, w_self, w_cross, w_ffn, gains, table, bucket_ids, block_order):
    row_count = tokens.shape[1]
    model_width = tokens.shape[2]
    head_count = table.shape[1]
    head_size = model_width // head_count
    hidden_units = w_ffn.shape[1] // 3
    block = row_count // 2
    seq_length = bucket_ids.shape[0]
    steps = seq_length // block
    ctx_place = lax.axis_index("ctx")
    fsdp_size = lax.axis_size("fsdp")
    small = jnp.concatenate([gains.reshape(1, -1), table.reshape(1, -1)], axis=1)
    far_small = far_rows(small)
    held_self = far_rows(w_self)
    held_self = near_rows(
        [(after(piece, *[other for other, _ in far_small[1:]]), at) for piece, at in held_self]
    )
    small_held = near_rows(far_small)
    small = jnp.zeros((fsdp_size, small.shape[1]), small.dtype)
    for piece, at in small_held:
        small = lax.dynamic_update_slice_in_dim(small, piece, at, 0)
    gain_rows = jnp.transpose(
        small[:, : gains.size].reshape((fsdp_size,) + gains.shape), (1, 0, 2)
    ).reshape(gains.shape[0], -1)
    table_rows = small[:, gains.size :].reshape(-1, head_count)
    row_pair = jnp.concatenate([tokens[0], encoded[0]], axis=0)
    row_pairs = lax.all_gather(row_pair, "ctx", axis=0, tiled=False)
    held_cross = far_rows(after(w_cross, small, *[piece for piece, _ in held_self[1:]]))
    held_ffn = far_rows(after(w_ffn, *[piece for piece, _ in held_cross[1:]]))
    whole_self = place_rows([piece for piece, _ in held_self], [at for _, at in held_self])
    gain_float = gain_rows.astype(jnp.float32)
    bucket_count = table_rows.shape[0]
    in_bucket = (
        bucket_ids[None, :] == jnp.arange(bucket_count, dtype=jnp.int32)[:, None]
    ).astype(jnp.float32)
    by_distance = lax.dot_general(
        table_rows.astype(jnp.float32),
        in_bucket,
        (((0,), (0,)), ((), ())),
        precision=lax.Precision.HIGHEST,
    )
    tiles = bias_tiles(
        after(distance_rows(by_distance, block), whole_self), LANES // head_size
    )
    own_blocks = lax.dynamic_slice_in_dim(block_order, 2 * ctx_place, 2)
    apart = own_blocks[:, None] - block_order[None, :]
    places = jnp.where(apart < 0, steps, apart).astype(jnp.int32).reshape(-1)

    inputs = tokens[0].astype(jnp.float32)
    held_cross = near_rows([(after(piece, tiles), at) for piece, at in held_cross])
    whole_cross = place_rows([piece for piece, _ in held_cross], [at for _, at in held_cross])
    row_pairs = after(row_pairs, whole_cross)
    encoder_all = row_pairs[:, row_count:].reshape(-1, model_width)
    normed_all = rounded(
        row_norm(row_pairs[:, :row_count].astype(jnp.float32), gain_float[0])
    ).reshape(-1, model_width)
    normed_one = rounded(row_norm(inputs, gain_float[0]))
    queries = rounded(dot(normed_one, whole_self[:, :model_width]))
    key_values = rounded(dot(normed_all, whole_self[:, model_width : 3 * model_width]))
    attended, weights, inverses = attention_forward(queries, key_values, head_size, tiles, places)
    held_ffn = near_rows([(after(piece, attended), at) for piece, at in held_ffn])
    encoder_kv = rounded(dot(encoder_all, whole_cross[:, model_width : 3 * model_width]))
    after_one = inputs + dot(attended, whole_self[:, 3 * model_width :])
    normed_two = rounded(row_norm(after_one, gain_float[1]))
    cross_query = rounded(dot(normed_two, whole_cross[:, :model_width]))
    cross_rows, cross_weights, cross_inverses = attention_forward(
        cross_query, encoder_kv, head_size
    )
    held_ffn = [(after(piece, cross_rows), at) for piece, at in held_ffn]
    whole_ffn = place_rows([piece for piece, _ in held_ffn], [at for _, at in held_ffn])
    after_two = after_one + dot(cross_rows, whole_cross[:, 3 * model_width :])
    normed_three = rounded(row_norm(after_two, gain_float[2]))
    gate_up = dot(normed_three, whole_ffn[:, : 2 * hidden_units])
    mixed_float, gated_back = jax.vjp(gated_gelu, gate_up)
    mixed_rows = rounded(mixed_float)
    output = rounded(after_two + dot_t(mixed_rows, whole_ffn[:, 2 * hidden_units :]))

    grad_branch_three = cotangent[0]
    grad_after_two = grad_branch_three.astype(jnp.float32)
    grad_mixed = dot(grad_branch_three, whole_ffn[:, 2 * hidden_units :])
    grad_gate_up = rounded(gated_back(grad_mixed)[0])
    grad_normed_three = dot_t(grad_gate_up, whole_ffn[:, : 2 * hidden_units])
    ffn_sum = Reduction(
        [
            Product(normed_three, grad_gate_up, fsdp_size),
            Product(grad_branch_three, mixed_rows, fsdp_size),
        ],
        "fsdp",
    )
    grad_normed_three = advance([ffn_sum], grad_normed_three)
    norm_part = jax.vjp(row_norm, after_two, gain_float[2])[1](grad_normed_three)[0]
    grad_after_one = grad_after_two + norm_part
    grad_branch_two = rounded(grad_after_one)
    grad_cross_rows = rounded(dot_t(grad_branch_two, whole_cross[:, 3 * model_width :]))
    grad_cross_rows = advance([ffn_sum], grad_cross_rows)
    grad_cross_query, encoder_full = attention_backward(
        cross_query, encoder_kv, grad_cross_rows, cross_rows, cross_weights, cross_inverses,
        head_size, False,
    )
    grad_normed_two = dot_t(grad_cross_query, whole_cross[:, :model_width])
    norm_part = jax.vjp(row_norm, after_one, gain_float[1])[1](grad_normed_two)[0]
    grad_inputs_one = grad_after_one + norm_part
    grad_branch_one = rounded(grad_inputs_one)
    grad_attended = rounded(dot_t(grad_branch_one, whole_self[:, 3 * model_width :]))
    cross_sum = Reduction(
        [
            Product(normed_two, grad_cross_query, fsdp_size),
            Product(encoder_all, encoder_full[0], fsdp_size),
            Product(encoder_all, encoder_full[1], fsdp_size),
            Product(cross_rows, grad_branch_two, fsdp_size),
        ],
        "fsdp",
    )
    grad_encoder_part = rounded(
        dot_t(encoder_full[0], whole_cross[:, model_width : 2 * model_width])
        + dot_t(encoder_full[1], whole_cross[:, 2 * model_width : 3 * model_width])
    )
    encoder_sum = Reduction([Ready(grad_encoder_part, 1)], "ctx")
    grad_attended = advance([cross_sum, encoder_sum], grad_attended)
    grad_query, grad_keys, distance_sums = attention_backward(
        queries, key_values, grad_attended, attended, weights, inverses, head_size, True
    )
    ffn_shard, grad_query, grad_keys, distance_sums = lax.optimization_barrier(
        (finish(ffn_sum), grad_query, grad_keys, distance_sums)
    )
    grad_query, grad_keys = advance([cross_sum], grad_query, grad_keys)
    ffn_shard = lax.psum_scatter(ffn_shard, "ctx", scatter_dimension=0, tiled=True)
    self_sum = Reduction(
        [
            Product(normed_one, grad_query, fsdp_size),
            Product(normed_all, grad_keys[0], fsdp_size),
            Product(normed_all, grad_keys[1], fsdp_size),
            Product(attended, grad_branch_one, fsdp_size),
        ],
        "fsdp",
    )
    grad_keys = advance([self_sum], grad_keys)
    key_weights = whole_self[:, model_width : 2 * model_width]
    value_weights = whole_self[:, 2 * model_width : 3 * model_width]
    grad_normed_part = rounded(
        dot_t(grad_keys[0], key_weights) + dot_t(grad_keys[1], value_weights)
    )
    token_sum = Reduction([Ready(grad_normed_part, 1)], "ctx")
    distance_sums = advance([token_sum, encoder_sum], distance_sums)
    cross_shard, distance_sums = lax.optimization_barrier((finish(cross_sum), distance_sums))
    distance_sums = advance([self_sum], distance_sums)
    in_place = (places[None, :] == jnp.arange(steps, dtype=jnp.int32)[:, None]).astype(jnp.float32)
    distance_sums = jnp.einsum(
        "sp,hpw->hsw", in_place, distance_sums, precision=lax.Precision.HIGHEST
    )
    grad_table = lax.dot_general(
        in_bucket,
        by_distance_sums(distance_sums, block),
        (((1,), (1,)), ((), ())),
        precision=lax.Precision.HIGHEST,
    )
    grad_normed_query = dot_t(grad_query, whole_self[:, :model_width])
    for bit in range(bit_count("fsdp")):
        grad_table = grad_table + swap(grad_table, "fsdp", bit)
    table_columns = jnp.pad(
        lax.dynamic_slice_in_dim(
            grad_table, lax.axis_index("fsdp") * table.shape[0], table.shape[0], 0
        ),
        ((0, gains.shape[1] - table.shape[0]), (0, LANES - head_count)),
    )
    rest = jnp.concatenate([cross_shard, finish(self_sum), rounded(table_columns)], axis=1)
    rest_sum = Reduction([Ready(rest, 1)], "ctx", "gather")
    sums = [rest_sum, token_sum, encoder_sum]
    while any(item.plan for item in sums):
        advance([item for item in sums if item.plan])
    ffn_rows = lax.all_gather(ffn_shard, "ctx", axis=0, tiled=True)
    grad_normed_one = grad_normed_query + token_sum.result().astype(jnp.float32)
    norm_part = jax.vjp(row_norm, inputs, gain_float[0])[1](grad_normed_one)[0]
    grad_tokens = rounded(grad_inputs_one + norm_part)
    grad_encoded = encoder_sum.result()
    ffn_grad = ffn_rows.astype(jnp.float32)
    rest = rest_sum.result().astype(jnp.float32)
    cross_grad = rest[:, : 4 * model_width]
    self_grad = rest[:, 4 * model_width : 8 * model_width]
    table_own = rest[: table.shape[0], 8 * model_width : 8 * model_width + head_count]
    gain_own = jnp.stack(
        [
            weighed(w_self[:, : 3 * model_width], self_grad),
            weighed(w_cross[:, :model_width], cross_grad),
            weighed(w_ffn[:, : 2 * hidden_units], ffn_grad),
        ]
    ) / gains.astype(jnp.float32)
    return (
        output[None],
        grad_tokens[None],
        grad_encoded[None],
        self_grad,
        cross_grad,
        ffn_grad,
        gain_own,
        table_own,
    )


def solution(mesh):
    in_specs = (
        P("fsdp", "ctx", None),
        P("fsdp", "ctx", None),
        P("fsdp", "ctx", None),
        P("fsdp", None),
        P("fsdp", None),
        P("fsdp", None),
        P(None, "fsdp"),
        P("fsdp", None),
        P(),
        P(),
    )
    out_specs = (
        P("fsdp", "ctx", None),
        P("fsdp", "ctx", None),
        P("fsdp", "ctx", None),
        P("fsdp", None),
        P("fsdp", None),
        P("fsdp", None),
        P(None, "fsdp"),
        P("fsdp", None),
    )
    return jax.shard_map(body, mesh=mesh, in_specs=in_specs, out_specs=out_specs, check_vma=False)
```

```python
import functools
import math

import jax
import jax.numpy as jnp
from jax import lax
from jax.experimental import pallas as pl
from jax.experimental.pallas import tpu as pltpu
from jax.sharding import PartitionSpec as P

NEGATIVE = -1e30
LANES = 128
VMEM_BYTES = 56 * 2**20


def dot(left, right):
    return lax.dot_general(
        left, right, (((1,), (0,)), ((), ())), preferred_element_type=jnp.float32
    )


def dot_t(left, right):
    return lax.dot_general(
        left, right, (((1,), (1,)), ((), ())), preferred_element_type=jnp.float32
    )


def t_dot(left, right):
    return lax.dot_general(
        left, right, (((0,), (0,)), ((), ())), preferred_element_type=jnp.float32
    )


def head_lanes(shape, head, head_size):
    lane = lax.broadcasted_iota(jnp.int32, shape, len(shape) - 1)
    return (lane >= head * head_size) & (lane < (head + 1) * head_size)


def only_head(values, head, head_size):
    return jnp.where(head_lanes(values.shape, head, head_size), values, jnp.zeros_like(values))


def tile_kernel(vector_ref, tile_ref):
    size = tile_ref.shape[-1]
    for head in range(vector_ref.shape[0]):
        for step in range(vector_ref.shape[1]):
            row = jnp.broadcast_to(
                vector_ref[head, step : step + 1, :], (size, 2 * size)
            )
            rolled = pltpu.roll(row, 0, 1, stride=1, stride_axis=0)
            tile_ref[head, step] = rolled[:, :size].astype(jnp.bfloat16)


def bias_tiles(vectors, group):
    head_count, steps, width = vectors.shape
    size = width // 2
    return pl.pallas_call(
        tile_kernel,
        grid=(head_count // group,),
        in_specs=[pl.BlockSpec((group, steps, width), lambda g: (g, 0, 0))],
        out_specs=pl.BlockSpec((group, steps, size, size), lambda g: (g, 0, 0, 0)),
        out_shape=jax.ShapeDtypeStruct((head_count, steps, size, size), jnp.bfloat16),
        compiler_params=pltpu.CompilerParams(vmem_limit_bytes=VMEM_BYTES),
        name="bias_tiles",
    )(vectors)


def forward_kernel(head_size, biased, *refs):
    if biased:
        place_ref, q_ref, k_ref, v_ref, tile_ref, out_ref, weight_ref, inverse_ref, score_ref = refs
    else:
        q_ref, k_ref, v_ref, out_ref, weight_ref, inverse_ref, score_ref = refs
    rows, key_total = q_ref.shape[0], k_ref.shape[0]
    group = q_ref.shape[1] // head_size
    piece = LANES
    out = jnp.zeros(q_ref.shape, jnp.float32)
    for head in range(group):
        query = only_head(q_ref[...], head, head_size)
        tops = [None] * (rows // piece)
        wide = 512
        for start in range(0, key_total, wide):
            scores = dot_t(query, k_ref[start : start + wide, :])
            for half in range(rows // piece):
                for part in range(wide // piece):
                    block = scores[
                        half * piece : (half + 1) * piece, part * piece : (part + 1) * piece
                    ]
                    key_block = start // piece + part
                    if biased:
                        place = place_ref[half * (key_total // piece) + key_block]
                        block = block + tile_ref[head, place].astype(jnp.float32)
                    score_ref[
                        half * piece : (half + 1) * piece,
                        key_block * piece : (key_block + 1) * piece,
                    ] = block
                    tops[half] = block if tops[half] is None else jnp.maximum(tops[half], block)
        top = jnp.concatenate([jnp.max(t, axis=1, keepdims=True) for t in tops], axis=0)
        total = jnp.zeros((rows, piece), jnp.float32)
        for start in range(0, key_total, piece):
            weights = jnp.exp(score_ref[:, start : start + piece] - top)
            total = total + weights
            weight_ref[head, :, start : start + piece] = weights.astype(jnp.bfloat16)
        inverse = 1.0 / jnp.sum(total, axis=1, keepdims=True)
        inverse_ref[head] = jnp.broadcast_to(inverse, (rows, LANES))
        mixed = dot(weight_ref[head], v_ref[...]) * inverse
        out = jnp.where(head_lanes(out.shape, head, head_size), mixed, out)
    out_ref[...] = out.astype(jnp.bfloat16)


def attention_forward(queries, key_values, head_size, tiles=None, places=None):
    rows, width = queries.shape
    key_total = key_values.shape[0]
    pairs = width // LANES
    group = LANES // head_size
    column = lambda shift: (lambda g, *_: (0, g + shift))
    in_specs = [
        pl.BlockSpec((rows, LANES), column(0)),
        pl.BlockSpec((key_total, LANES), column(0)),
        pl.BlockSpec((key_total, LANES), column(pairs)),
    ]
    operands = [queries, key_values, key_values]
    if tiles is not None:
        in_specs.append(
            pl.BlockSpec((group,) + tiles.shape[1:], lambda g, *_: (g, 0, 0, 0))
        )
        operands.append(tiles)
    grid_spec = pltpu.PrefetchScalarGridSpec(
        num_scalar_prefetch=0 if tiles is None else 1,
        grid=(pairs,),
        in_specs=in_specs,
        out_specs=[
            pl.BlockSpec((rows, LANES), column(0)),
            pl.BlockSpec((group, rows, key_total), lambda g, *_: (g, 0, 0)),
            pl.BlockSpec((group, rows, LANES), lambda g, *_: (g, 0, 0)),
        ],
        scratch_shapes=[pltpu.VMEM((rows, key_total), jnp.float32)],
    )
    heads = width // head_size
    return pl.pallas_call(
        functools.partial(forward_kernel, head_size, tiles is not None),
        grid_spec=grid_spec,
        out_shape=[
            jax.ShapeDtypeStruct((rows, width), jnp.bfloat16),
            jax.ShapeDtypeStruct((heads, rows, key_total), jnp.bfloat16),
            jax.ShapeDtypeStruct((heads, rows, LANES), jnp.float32),
        ],
        compiler_params=pltpu.CompilerParams(vmem_limit_bytes=VMEM_BYTES),
        cost_estimate=pl.CostEstimate(flops=1, bytes_accessed=1, transcendentals=0),
        name="attention_forward",
    )(*(() if places is None else (places,)), *operands)


def backward_kernel(head_size, biased, *refs):
    if biased:
        (q_ref, k_ref, v_ref, grad_ref, out_ref, weight_ref, inverse_ref,
         dq_ref, dkv_ref, dist_ref, ds_ref) = refs
    else:
        (q_ref, k_ref, v_ref, grad_ref, out_ref, weight_ref, inverse_ref,
         dq_ref, dkv_ref, ds_ref) = refs
    rows, key_total = q_ref.shape[0], k_ref.shape[0]
    group = q_ref.shape[1] // head_size
    piece = LANES
    wide = 512
    dq = jnp.zeros(q_ref.shape, jnp.float32)
    grads = grad_ref[...].astype(jnp.float32)
    deltas = grads * out_ref[...].astype(jnp.float32)
    scaled_all = []
    for head in range(group):
        inverse = inverse_ref[head]
        scaled = only_head((grads * inverse).astype(jnp.bfloat16), head, head_size)
        scaled_all.append(scaled)
        delta = jnp.sum(only_head(deltas, head, head_size), axis=1, keepdims=True) * inverse
        for start in range(0, key_total, wide):
            grad_probs = dot_t(scaled, v_ref[start : start + wide, :])
            for half in range(rows // piece):
                for part in range(wide // piece):
                    lo = half * piece
                    at = start + part * piece
                    block = grad_probs[lo : lo + piece, part * piece : (part + 1) * piece]
                    weights = weight_ref[head, lo : lo + piece, at : at + piece]
                    change = weights.astype(jnp.float32) * (block - delta[lo : lo + piece])
                    ds_ref[head * rows + lo : head * rows + lo + piece, at : at + piece] = (
                        change.astype(jnp.bfloat16)
                    )
        mixed = dot(ds_ref[head * rows : (head + 1) * rows, :], k_ref[...])
        dq = jnp.where(head_lanes(dq.shape, head, head_size), mixed, dq)
    dq_ref[...] = dq.astype(jnp.bfloat16)
    queries = jnp.concatenate(
        [only_head(q_ref[...], head, head_size) for head in range(group)], axis=0
    )
    scaled_rows = jnp.concatenate(scaled_all, axis=0)
    for start in range(0, key_total, wide):
        dkv_ref[0, start : start + wide, :] = t_dot(
            ds_ref[:, start : start + wide], queries
        ).astype(jnp.bfloat16)
        weights = jnp.concatenate(
            [weight_ref[head, :, start : start + wide] for head in range(group)], axis=0
        )
        dkv_ref[1, start : start + wide, :] = t_dot(weights, scaled_rows).astype(
            jnp.bfloat16
        )
    if biased:
        down = lax.broadcasted_iota(jnp.int32, (piece, piece), 0)
        across = lax.broadcasted_iota(jnp.int32, (piece, piece), 1)
        flip = (down + across == piece - 1).astype(jnp.bfloat16)
        for head in range(group):
            for half in range(rows // piece):
                lo = head * rows + half * piece
                for start in range(0, key_total, wide):
                    turned = dot(flip, ds_ref[lo : lo + piece, start : start + wide])
                    for part in range(wide // piece):
                        block = turned[:, part * piece : (part + 1) * piece]
                        rolled = pltpu.roll(block, 1, 1, stride=1, stride_axis=0)
                        later = jnp.sum(
                            jnp.where(across <= down, rolled, 0.0), axis=0, keepdims=True
                        )
                        every = jnp.sum(rolled, axis=0, keepdims=True)
                        at = half * (key_total // piece) + start // piece + part
                        dist_ref[head, at : at + 1, :piece] = later
                        dist_ref[head, at : at + 1, piece:] = every - later


def attention_backward(
    queries, key_values, grads, outs, weights, inverses, head_size, biased, first=0, count=None
):
    rows, width = queries.shape
    key_total = key_values.shape[0]
    pairs = width // LANES
    count = pairs if count is None else count
    group = LANES // head_size
    column = lambda shift: (lambda g: (0, g + shift))
    head_block = lambda g: (g + first, 0, 0)
    row_block = pl.BlockSpec((rows, LANES), column(first))
    blocks = rows // LANES * (key_total // LANES)
    out_specs = [
        pl.BlockSpec((rows, LANES), column(0)),
        pl.BlockSpec((2, key_total, LANES), lambda g: (0, 0, g)),
    ]
    out_shape = [
        jax.ShapeDtypeStruct((rows, count * LANES), jnp.bfloat16),
        jax.ShapeDtypeStruct((2, key_total, count * LANES), jnp.bfloat16),
    ]
    if biased:
        out_specs.append(pl.BlockSpec((group, blocks, 2 * LANES), lambda g: (g, 0, 0)))
        out_shape.append(
            jax.ShapeDtypeStruct((group * count, blocks, 2 * LANES), jnp.float32)
        )
    return pl.pallas_call(
        functools.partial(backward_kernel, head_size, biased),
        grid=(count,),
        in_specs=[
            row_block,
            pl.BlockSpec((key_total, LANES), column(first)),
            pl.BlockSpec((key_total, LANES), column(first + pairs)),
            row_block,
            row_block,
            pl.BlockSpec((group, rows, key_total), head_block),
            pl.BlockSpec((group, rows, LANES), head_block),
        ],
        out_specs=out_specs,
        out_shape=out_shape,
        scratch_shapes=[pltpu.VMEM((group * rows, key_total), jnp.bfloat16)],
        compiler_params=pltpu.CompilerParams(vmem_limit_bytes=VMEM_BYTES),
        cost_estimate=pl.CostEstimate(flops=1, bytes_accessed=1, transcendentals=0),
        name="attention_backward",
    )(queries, key_values, key_values, grads, outs, weights, inverses)


def place_kernel(count, at_ref, *refs):
    pieces, whole_ref, held_ref, in_sems, out_sems = refs[:count], *refs[count:]
    rows = held_ref.shape[1]
    parts = in_sems.shape[1]
    width = held_ref.shape[2] // parts
    loads, stores = [], []
    for index in range(count):
        start = pl.multiple_of(at_ref[index] * rows, rows)
        for part in range(parts):
            columns = pl.ds(part * width, width)
            held = held_ref.at[index, :, columns]
            loads.append(
                pltpu.make_async_copy(
                    pieces[index].at[:, columns], held, in_sems.at[index, part]
                )
            )
            stores.append(
                pltpu.make_async_copy(
                    held, whole_ref.at[pl.ds(start, rows), columns], out_sems.at[index, part]
                )
            )
    for load in loads:
        load.start()
    for load, store in zip(loads, stores):
        load.wait()
        store.start()
    for store in stores:
        store.wait()


def place_rows(pieces, places):
    rows, width = pieces[0].shape
    count = len(pieces)
    parts = width // 1024
    return pl.pallas_call(
        functools.partial(place_kernel, count),
        grid_spec=pltpu.PrefetchScalarGridSpec(
            num_scalar_prefetch=1,
            grid=(1,),
            in_specs=[pl.BlockSpec(memory_space=pl.ANY)] * count,
            out_specs=pl.BlockSpec(memory_space=pl.ANY),
            scratch_shapes=[
                pltpu.VMEM((count, rows, width), pieces[0].dtype),
                pltpu.SemaphoreType.DMA((count, parts)),
                pltpu.SemaphoreType.DMA((count, parts)),
            ],
        ),
        out_shape=jax.ShapeDtypeStruct((rows * count, width), pieces[0].dtype),
        compiler_params=pltpu.CompilerParams(vmem_limit_bytes=VMEM_BYTES),
        name="place_rows",
    )(jnp.stack(places).astype(jnp.int32), *pieces)


class Part:
    def __init__(self, array, chosen=()):
        self.array = array
        self.chosen = chosen

    def take(self, bit):
        return Part(self.array, (bit,) + self.chosen)

    def lead(self):
        return (2,) * (self.array.ndim - 2 - len(self.chosen))

    def rows(self):
        return math.prod(self.lead()) * self.array.shape[-2]

    def block(self, width):
        return self.lead() + (1,) * len(self.chosen) + (self.array.shape[-2], width)

    def start(self, places, first):
        whole = len(self.lead())
        return (0,) * whole + tuple(places[first + i] for i in range(len(self.chosen)))


def products_kernel(spans, place_ref, *refs):
    count = len(spans)
    lefts, rights, adds, out_ref = refs[:count], refs[count : 2 * count], refs[2 * count : -1], refs[-1]
    flat = lambda values: values.reshape(-1, values.shape[-1])
    step = pl.program_id(0)
    for index, (first, last) in enumerate(spans):

        @pl.when((step >= first) & (step < last))
        def _(index=index):
            total = dot(flat(lefts[index][...]), rights[index][...])
            for add in adds:
                total = total + flat(add[...]).astype(jnp.float32)
            out_ref[...] = total.astype(jnp.bfloat16)


def products(lefts, rights, adds):
    rows = lefts[0].rows()
    widths = [right.shape[1] for right in rights]
    tile = math.gcd(*widths)
    while tile > 1024:
        tile //= 2
    spans, first = [], 0
    for width in widths:
        spans.append((first, first + width // tile))
        first += width // tile
    places, starts = [jnp.int32(0)], []
    for part in lefts + adds:
        starts.append(len(places))
        places += list(part.chosen)

    def left_spec(part, at):
        return pl.BlockSpec(
            part.block(part.array.shape[-1]),
            lambda step, place_ref: part.start(place_ref, at) + (0, 0),
        )

    def add_spec(part, at):
        return pl.BlockSpec(
            part.block(tile), lambda step, place_ref: part.start(place_ref, at) + (0, step)
        )

    def right_spec(right, span):
        lo, hi = span
        return pl.BlockSpec(
            (right.shape[0], tile),
            lambda step, place_ref: (0, jnp.clip(step - lo, 0, hi - lo - 1)),
        )

    count = len(lefts)
    total = pl.pallas_call(
        functools.partial(products_kernel, spans),
        grid_spec=pltpu.PrefetchScalarGridSpec(
            num_scalar_prefetch=1,
            grid=(first,),
            in_specs=[left_spec(part, at) for part, at in zip(lefts, starts[:count])]
            + [right_spec(right, span) for right, span in zip(rights, spans)]
            + [add_spec(part, at) for part, at in zip(adds, starts[count:])],
            out_specs=pl.BlockSpec((rows, tile), lambda step, place_ref: (0, step)),
        ),
        out_shape=jax.ShapeDtypeStruct((rows, sum(widths)), jnp.bfloat16),
        compiler_params=pltpu.CompilerParams(vmem_limit_bytes=VMEM_BYTES),
        cost_estimate=pl.CostEstimate(flops=1, bytes_accessed=1, transcendentals=0),
        name="products",
    )(
        jnp.stack([jnp.asarray(place, jnp.int32) for place in places]),
        *[part.array for part in lefts],
        *rights,
        *[part.array for part in adds],
    )
    return total.reshape(lefts[0].lead() + (-1, total.shape[1]))


def back_kernel(grad_ref, key_weight_ref, value_weight_ref, out_ref):
    total = dot_t(grad_ref[0], key_weight_ref[...]) + dot_t(grad_ref[1], value_weight_ref[...])
    out_ref[...] = total.astype(jnp.bfloat16)


def back_to_rows(grads, weights, width):
    rows = grads.shape[1]
    tile = math.gcd(rows, 512)
    return pl.pallas_call(
        back_kernel,
        grid=(rows // tile,),
        in_specs=[
            pl.BlockSpec((2, tile, width), lambda step: (0, step, 0)),
            pl.BlockSpec((width, width), lambda step: (0, 1)),
            pl.BlockSpec((width, width), lambda step: (0, 2)),
        ],
        out_specs=pl.BlockSpec((tile, width), lambda step: (step, 0)),
        out_shape=jax.ShapeDtypeStruct((rows, width), jnp.bfloat16),
        compiler_params=pltpu.CompilerParams(vmem_limit_bytes=VMEM_BYTES),
        cost_estimate=pl.CostEstimate(flops=1, bytes_accessed=1, transcendentals=0),
        name="back_to_rows",
    )(grads, weights, weights)


EPSILON = 1e-06


def row_norm(values, gain):
    return values * lax.rsqrt(jnp.mean(values * values, axis=-1, keepdims=True) + EPSILON) * gain


def gated_gelu(gate_up):
    hidden_units = gate_up.shape[1] // 2
    return jax.nn.gelu(gate_up[:, :hidden_units], approximate=True) * gate_up[:, hidden_units:]


def rounded(values):
    return values.astype(jnp.bfloat16)


def distance_rows(by_distance, block):
    heads = by_distance.shape[0]
    padded = jnp.concatenate(
        [
            jnp.full((heads, block - 1), NEGATIVE, jnp.float32),
            by_distance,
            jnp.full((heads, 1), NEGATIVE, jnp.float32),
        ],
        axis=1,
    )
    pieces = padded.reshape(heads, -1, block)[:, :, ::-1]
    rows = jnp.concatenate([pieces[:, :-1], pieces[:, 1:]], axis=2)
    return jnp.concatenate([rows, jnp.full((heads, 1, 2 * block), NEGATIVE, jnp.float32)], axis=1)


def by_distance_sums(rows, block):
    heads, steps, _ = rows.shape
    zero = jnp.zeros((heads, 1, block), jnp.float32)
    pieces = jnp.concatenate([rows[:, :, :block], zero], axis=1) + jnp.concatenate(
        [zero, rows[:, :, block:]], axis=1
    )
    return pieces[:, :, ::-1].reshape(heads, -1)[:, block - 1 : block - 1 + steps * block]


def bit_count(axis_name):
    return int(math.log2(lax.axis_size(axis_name)))


def swap(values, axis_name, bit):
    size = lax.axis_size(axis_name)
    return lax.ppermute(values, axis_name, [(i, i ^ (1 << bit)) for i in range(size)])


def own_bit(axis_name, bit):
    return (lax.axis_index(axis_name) >> bit) & 1


def pick(values, index, axis):
    return lax.dynamic_index_in_dim(values, index, axis, keepdims=False)


def after(value, *others):
    return lax.optimization_barrier((value,) + others)[0]


def far_rows(share):
    held = [(share, lax.axis_index("fsdp"))]
    for bit in reversed(range(1, bit_count("fsdp"))):
        held = held + [(swap(piece, "fsdp", bit), at ^ (1 << bit)) for piece, at in held]
    return held


def near_rows(held):
    return held + [(swap(piece, "fsdp", 0), at ^ 1) for piece, at in held]


def whole_rows(held):
    held = near_rows(held)
    return place_rows([piece for piece, _ in held], [at for _, at in held])


class Product:
    def __init__(self, left, right, parts):
        bits = int(math.log2(parts))
        self.left = Part(
            jnp.transpose(left).reshape(
                (2,) * bits + (left.shape[1] // parts, left.shape[0])
            )
        )
        self.right = right

    def take(self, bit):
        part = Product.__new__(Product)
        part.left = self.left.take(bit)
        part.right = self.right
        return part


class Ready:
    def __init__(self, values, parts):
        bits = int(math.log2(parts))
        self.values = values.reshape(
            (2,) * bits + (values.shape[0] // parts, values.shape[1])
        )

    def take(self, bit):
        part = Ready.__new__(Ready)
        part.values = pick(self.values, bit, self.values.ndim - 3)
        return part

    def value(self):
        return self.values


def joined(own, other, mine):
    return jnp.where(
        mine == 0, jnp.stack([own, other], axis=-3), jnp.stack([other, own], axis=-3)
    )


class Reduction:
    def __init__(self, terms, *stages):
        self.terms = terms
        self.received = []
        self.kept = None
        self.pending = None
        self.gathered = None
        self.plan = []
        for stage in stages:
            bits = [(stage, bit) for bit in range(bit_count("fsdp" if stage == "fsdp" else "ctx"))]
            self.plan += reversed(bits) if stage == "gather" else bits

    def shard(self):
        return self.added(self.terms, self.received)

    def added(self, terms, received):
        if isinstance(terms[0], Ready):
            return terms[0].value()
        return products(
            [term.left for term in terms], [term.right for term in terms], received
        )

    def merged(self):
        if self.gathered is not None:
            own, bit = self.gathered
            return joined(own, self.pending, own_bit("ctx", bit))
        if self.kept is not None:
            return rounded(self.kept.astype(jnp.float32) + self.pending.astype(jnp.float32))
        total = self.shard()
        parts = lax.axis_size("ctx")
        return total.reshape(
            (2,) * bit_count("ctx") + (total.shape[0] // parts, total.shape[1])
        )

    def settle(self, main):
        main = tuple(main)
        if self.pending is not None:
            self.pending, *main = lax.optimization_barrier((self.pending,) + main)
        elif self.received:
            arrays = tuple(part.array for part in self.received)
            arrays, main = lax.optimization_barrier((arrays, main))
            self.received = [
                Part(array, part.chosen) for array, part in zip(arrays, self.received)
            ]
        return tuple(main)

    def prepare(self):
        kind, bit = self.step = self.plan.pop(0)
        if kind == "gather":
            total = self.merged()
            self.gathered = (total, bit)
            return total
        mine = own_bit(kind, bit)
        if kind == "ctx":
            total = self.merged()
            self.kept = pick(total, mine, total.ndim - 3)
            return pick(total, 1 - mine, total.ndim - 3)
        send = self.added(
            [term.take(1 - mine) for term in self.terms],
            [item.take(1 - mine) for item in self.received],
        )
        self.terms = [term.take(mine) for term in self.terms]
        self.received = [item.take(mine) for item in self.received]
        return send

    def exchange(self, send):
        kind, bit = self.step
        other = swap(send, "fsdp" if kind == "fsdp" else "ctx", bit)
        if kind == "fsdp":
            self.received.append(Part(other))
        else:
            self.pending = other

    def result(self):
        total = self.merged()
        return total.reshape(-1, total.shape[-1])


class Gathering(Reduction):
    def __init__(self, rows):
        super().__init__([Ready(rows, 1)], "gather")

    def merged(self):
        return super().merged() if self.gathered is not None else self.shard()


def finish(item):
    while item.plan:
        advance([item])
    return item.shard()


def advance(sums, *main):
    if main:
        for item in sums:
            main = item.settle(main)
    sends = [item.prepare() for item in sums]
    held = lax.optimization_barrier(tuple(sends) + tuple(main))
    for item, send in zip(sums, held):
        item.exchange(send)
    main = held[len(sums) :]
    return main[0] if len(main) == 1 else main


def weighed(weight, grad):
    return jnp.sum(weight.astype(jnp.float32) * grad[:, : weight.shape[1]], axis=1)


def body(tokens, encoded, cotangent, w_self, w_cross, w_ffn, gains, table, bucket_ids, block_order):
    row_count = tokens.shape[1]
    model_width = tokens.shape[2]
    head_count = table.shape[1]
    head_size = model_width // head_count
    hidden_units = w_ffn.shape[1] // 3
    block = row_count // 2
    seq_length = bucket_ids.shape[0]
    steps = seq_length // block
    ctx_place = lax.axis_index("ctx")
    fsdp_size = lax.axis_size("fsdp")
    small = jnp.concatenate([gains.reshape(1, -1), table.reshape(1, -1)], axis=1)
    far_small = far_rows(small)
    held_self = far_rows(w_self)
    held_self = near_rows(
        [(after(piece, *[other for other, _ in far_small[1:]]), at) for piece, at in held_self]
    )
    small_held = near_rows(far_small)
    small = jnp.zeros((fsdp_size, small.shape[1]), small.dtype)
    for piece, at in small_held:
        small = lax.dynamic_update_slice_in_dim(small, piece, at, 0)
    gain_rows = jnp.transpose(
        small[:, : gains.size].reshape((fsdp_size,) + gains.shape), (1, 0, 2)
    ).reshape(gains.shape[0], -1)
    table_rows = small[:, gains.size :].reshape(-1, head_count)
    token_rows = lax.all_gather(tokens[0], "ctx", axis=0, tiled=True)
    encoder_sum = Gathering(encoded[0])
    advance([encoder_sum])
    held_cross = far_rows(after(w_cross, small, *[piece for piece, _ in held_self[1:]]))
    held_ffn = far_rows(after(w_ffn, *[piece for piece, _ in held_cross[1:]]))
    whole_self = place_rows([piece for piece, _ in held_self], [at for _, at in held_self])
    encoder_sum.pending = after(encoder_sum.pending, whole_self[:8, :LANES])
    advance([encoder_sum])
    gain_float = gain_rows.astype(jnp.float32)
    bucket_count = table_rows.shape[0]
    in_bucket = (
        bucket_ids[None, :] == jnp.arange(bucket_count, dtype=jnp.int32)[:, None]
    ).astype(jnp.float32)
    by_distance = lax.dot_general(
        table_rows.astype(jnp.float32),
        in_bucket,
        (((0,), (0,)), ((), ())),
        precision=lax.Precision.HIGHEST,
    )
    tiles = bias_tiles(
        after(distance_rows(by_distance, block), whole_self), LANES // head_size
    )
    own_blocks = lax.dynamic_slice_in_dim(block_order, 2 * ctx_place, 2)
    apart = own_blocks[:, None] - block_order[None, :]
    places = jnp.where(apart < 0, steps, apart).astype(jnp.int32).reshape(-1)

    inputs = tokens[0].astype(jnp.float32)
    gain_first = after(gain_float[0], tiles)
    normed_all = rounded(row_norm(token_rows.astype(jnp.float32), gain_first))
    normed_all = advance([encoder_sum], normed_all)
    normed_one = rounded(row_norm(inputs, gain_float[0]))
    queries = rounded(dot(normed_one, whole_self[:, :model_width]))
    key_values = rounded(dot(normed_all, whole_self[:, model_width : 3 * model_width]))
    held_cross = near_rows([(after(piece, normed_one), at) for piece, at in held_cross])
    attended, weights, inverses = attention_forward(queries, key_values, head_size, tiles, places)
    held_cross = [(after(piece, attended), at) for piece, at in held_cross]
    whole_cross = place_rows([piece for piece, _ in held_cross], [at for _, at in held_cross])
    after_one = inputs + dot(attended, whole_self[:, 3 * model_width :])
    normed_two = rounded(row_norm(after_one, gain_float[1]))
    cross_query = rounded(dot(normed_two, whole_cross[:, :model_width]))
    cross_query = encoder_sum.settle((cross_query,))[0]
    while encoder_sum.plan:
        cross_query = advance([encoder_sum], cross_query)
    encoder_all = encoder_sum.result()
    encoder_kv = rounded(dot(encoder_all, whole_cross[:, model_width : 3 * model_width]))
    held_ffn = near_rows([(after(piece, encoder_kv), at) for piece, at in held_ffn])
    cross_rows, cross_weights, cross_inverses = attention_forward(
        cross_query, encoder_kv, head_size
    )
    held_ffn = [(after(piece, cross_rows), at) for piece, at in held_ffn]
    whole_ffn = place_rows([piece for piece, _ in held_ffn], [at for _, at in held_ffn])
    after_two = after_one + dot(cross_rows, whole_cross[:, 3 * model_width :])
    normed_three = rounded(row_norm(after_two, gain_float[2]))
    gate_up = dot(normed_three, whole_ffn[:, : 2 * hidden_units])
    mixed_float, gated_back = jax.vjp(gated_gelu, gate_up)
    mixed_rows = rounded(mixed_float)
    output = rounded(after_two + dot_t(mixed_rows, whole_ffn[:, 2 * hidden_units :]))

    grad_branch_three = cotangent[0]
    grad_after_two = grad_branch_three.astype(jnp.float32)
    grad_mixed = dot(grad_branch_three, whole_ffn[:, 2 * hidden_units :])
    grad_gate_up = rounded(gated_back(grad_mixed)[0])
    grad_normed_three = dot_t(grad_gate_up, whole_ffn[:, : 2 * hidden_units])
    ffn_sum = Reduction(
        [
            Product(normed_three, grad_gate_up, fsdp_size),
            Product(grad_branch_three, mixed_rows, fsdp_size),
        ],
        "fsdp",
    )
    grad_normed_three = advance([ffn_sum], grad_normed_three)
    norm_part = jax.vjp(row_norm, after_two, gain_float[2])[1](grad_normed_three)[0]
    grad_after_one = grad_after_two + norm_part
    grad_branch_two = rounded(grad_after_one)
    grad_cross_rows = rounded(dot_t(grad_branch_two, whole_cross[:, 3 * model_width :]))
    grad_cross_rows = advance([ffn_sum], grad_cross_rows)
    grad_cross_query, encoder_full = attention_backward(
        cross_query, encoder_kv, grad_cross_rows, cross_rows, cross_weights, cross_inverses,
        head_size, False,
    )
    grad_normed_two = dot_t(grad_cross_query, whole_cross[:, :model_width])
    norm_part = jax.vjp(row_norm, after_one, gain_float[1])[1](grad_normed_two)[0]
    grad_inputs_one = grad_after_one + norm_part
    grad_branch_one = rounded(grad_inputs_one)
    grad_attended = rounded(dot_t(grad_branch_one, whole_self[:, 3 * model_width :]))
    cross_sum = Reduction(
        [
            Product(normed_two, grad_cross_query, fsdp_size),
            Product(encoder_all, encoder_full[0], fsdp_size),
            Product(encoder_all, encoder_full[1], fsdp_size),
            Product(cross_rows, grad_branch_two, fsdp_size),
        ],
        "fsdp",
    )
    grad_encoder_part = back_to_rows(encoder_full, whole_cross, model_width)
    encoder_back = Reduction([Ready(grad_encoder_part, 1)], "ctx")
    grad_attended = advance([cross_sum, encoder_back], grad_attended)
    grad_query, grad_keys, distance_sums = attention_backward(
        queries, key_values, grad_attended, attended, weights, inverses, head_size, True
    )
    ffn_shard, grad_query, grad_keys, distance_sums = lax.optimization_barrier(
        (finish(ffn_sum), grad_query, grad_keys, distance_sums)
    )
    grad_query, grad_keys = advance([cross_sum], grad_query, grad_keys)
    ffn_shard = lax.psum_scatter(ffn_shard, "ctx", scatter_dimension=0, tiled=True)
    self_sum = Reduction(
        [
            Product(normed_one, grad_query, fsdp_size),
            Product(normed_all, grad_keys[0], fsdp_size),
            Product(normed_all, grad_keys[1], fsdp_size),
            Product(attended, grad_branch_one, fsdp_size),
        ],
        "fsdp",
    )
    grad_keys = advance([self_sum], grad_keys)
    key_weights = whole_self[:, model_width : 2 * model_width]
    value_weights = whole_self[:, 2 * model_width : 3 * model_width]
    grad_normed_part = back_to_rows(grad_keys, whole_self, model_width)
    token_sum = Reduction([Ready(grad_normed_part, 1)], "ctx")
    distance_sums = advance([self_sum], distance_sums)
    distance_sums = cross_sum.settle((distance_sums,))[0]
    distance_sums = advance([token_sum, encoder_back], distance_sums)
    in_place = (places[None, :] == jnp.arange(steps, dtype=jnp.int32)[:, None]).astype(jnp.float32)
    distance_sums = jnp.einsum(
        "sp,hpw->hsw", in_place, distance_sums, precision=lax.Precision.HIGHEST
    )
    grad_table = lax.dot_general(
        in_bucket,
        by_distance_sums(distance_sums, block),
        (((1,), (1,)), ((), ())),
        precision=lax.Precision.HIGHEST,
    )
    grad_normed_query = dot_t(grad_query, whole_self[:, :model_width])
    cross_rest = Reduction([Ready(finish(cross_sum), 1)], "ctx", "gather")
    grad_table = advance([cross_rest], grad_table)
    for bit in range(bit_count("fsdp")):
        grad_table = grad_table + swap(grad_table, "fsdp", bit)
    table_columns = jnp.pad(
        lax.dynamic_slice_in_dim(
            grad_table, lax.axis_index("fsdp") * table.shape[0], table.shape[0], 0
        ),
        ((0, gains.shape[1] - table.shape[0]), (0, LANES - head_count)),
    )
    rest = jnp.concatenate([finish(self_sum), rounded(table_columns)], axis=1)
    ahead = [token_sum, encoder_back, cross_rest]
    rest = advance(ahead, rest)
    ffn_shard, rest = lax.optimization_barrier((ffn_shard, rest))
    ffn_rows = lax.all_gather(ffn_shard, "ctx", axis=0, tiled=True)
    rest_sum = Reduction([Ready(rest, 1)], "ctx", "gather")
    advance([rest_sum])
    while rest_sum.plan:
        ahead = [item for item in ahead if item.plan]
        if ahead:
            rest_sum.pending = advance(ahead, rest_sum.pending)
        if len(rest_sum.plan) == bit_count("ctx"):
            rest_sum.pending, ffn_rows = lax.optimization_barrier((rest_sum.pending, ffn_rows))
        advance([rest_sum])
    while any(item.plan for item in ahead):
        advance([item for item in ahead if item.plan])
    grad_normed_one = grad_normed_query + token_sum.result().astype(jnp.float32)
    norm_part = jax.vjp(row_norm, inputs, gain_float[0])[1](grad_normed_one)[0]
    grad_tokens = rounded(grad_inputs_one + norm_part)
    grad_encoded = encoder_back.result()
    ffn_grad = ffn_rows.astype(jnp.float32)
    cross_grad = cross_rest.result().astype(jnp.float32)
    rest = rest_sum.result().astype(jnp.float32)
    self_grad = rest[:, : 4 * model_width]
    table_own = rest[: table.shape[0], 4 * model_width : 4 * model_width + head_count]
    gain_own = jnp.stack(
        [
            weighed(w_self[:, : 3 * model_width], self_grad),
            weighed(w_cross[:, :model_width], cross_grad),
            weighed(w_ffn[:, : 2 * hidden_units], ffn_grad),
        ]
    ) / gains.astype(jnp.float32)
    return (
        output[None],
        grad_tokens[None],
        grad_encoded[None],
        self_grad,
        cross_grad,
        ffn_grad,
        gain_own,
        table_own,
    )


def solution(mesh):
    in_specs = (
        P("fsdp", "ctx", None),
        P("fsdp", "ctx", None),
        P("fsdp", "ctx", None),
        P("fsdp", None),
        P("fsdp", None),
        P("fsdp", None),
        P(None, "fsdp"),
        P("fsdp", None),
        P(),
        P(),
    )
    out_specs = (
        P("fsdp", "ctx", None),
        P("fsdp", "ctx", None),
        P("fsdp", "ctx", None),
        P("fsdp", None),
        P("fsdp", None),
        P("fsdp", None),
        P(None, "fsdp"),
        P("fsdp", None),
    )
    return jax.shard_map(body, mesh=mesh, in_specs=in_specs, out_specs=out_specs, check_vma=False)
```

```python
import functools
import math

import jax
import jax.numpy as jnp
from jax import lax
from jax.experimental import pallas as pl
from jax.experimental.pallas import tpu as pltpu
from jax.sharding import PartitionSpec as P

NEGATIVE = -1e30
LANES = 128
VMEM_BYTES = 56 * 2**20


def dot(left, right):
    return lax.dot_general(
        left, right, (((1,), (0,)), ((), ())), preferred_element_type=jnp.float32
    )


def dot_t(left, right):
    return lax.dot_general(
        left, right, (((1,), (1,)), ((), ())), preferred_element_type=jnp.float32
    )


def t_dot(left, right):
    return lax.dot_general(
        left, right, (((0,), (0,)), ((), ())), preferred_element_type=jnp.float32
    )


def head_lanes(shape, head, head_size):
    lane = lax.broadcasted_iota(jnp.int32, shape, len(shape) - 1)
    return (lane >= head * head_size) & (lane < (head + 1) * head_size)


def only_head(values, head, head_size):
    return jnp.where(head_lanes(values.shape, head, head_size), values, jnp.zeros_like(values))


def tile_kernel(vector_ref, tile_ref):
    size = tile_ref.shape[-1]
    for head in range(vector_ref.shape[0]):
        for step in range(vector_ref.shape[1]):
            row = jnp.broadcast_to(
                vector_ref[head, step : step + 1, :], (size, 2 * size)
            )
            rolled = pltpu.roll(row, 0, 1, stride=1, stride_axis=0)
            tile_ref[head, step] = rolled[:, :size].astype(jnp.bfloat16)


def bias_tiles(vectors, group):
    head_count, steps, width = vectors.shape
    size = width // 2
    return pl.pallas_call(
        tile_kernel,
        grid=(head_count // group,),
        in_specs=[pl.BlockSpec((group, steps, width), lambda g: (g, 0, 0))],
        out_specs=pl.BlockSpec((group, steps, size, size), lambda g: (g, 0, 0, 0)),
        out_shape=jax.ShapeDtypeStruct((head_count, steps, size, size), jnp.bfloat16),
        compiler_params=pltpu.CompilerParams(vmem_limit_bytes=VMEM_BYTES),
        name="bias_tiles",
    )(vectors)


def forward_kernel(head_size, biased, *refs):
    if biased:
        place_ref, q_ref, k_ref, v_ref, tile_ref, out_ref, weight_ref, inverse_ref, score_ref = refs
    else:
        q_ref, k_ref, v_ref, out_ref, weight_ref, inverse_ref, score_ref = refs
    rows, key_total = q_ref.shape[0], k_ref.shape[0]
    group = q_ref.shape[1] // head_size
    piece = LANES
    out = jnp.zeros(q_ref.shape, jnp.float32)
    for head in range(group):
        query = only_head(q_ref[...], head, head_size)
        tops = [None] * (rows // piece)
        wide = 512
        for start in range(0, key_total, wide):
            scores = dot_t(query, k_ref[start : start + wide, :])
            for half in range(rows // piece):
                for part in range(wide // piece):
                    block = scores[
                        half * piece : (half + 1) * piece, part * piece : (part + 1) * piece
                    ]
                    key_block = start // piece + part
                    if biased:
                        place = place_ref[half * (key_total // piece) + key_block]
                        block = block + tile_ref[head, place].astype(jnp.float32)
                    score_ref[
                        half * piece : (half + 1) * piece,
                        key_block * piece : (key_block + 1) * piece,
                    ] = block
                    tops[half] = block if tops[half] is None else jnp.maximum(tops[half], block)
        top = jnp.concatenate([jnp.max(t, axis=1, keepdims=True) for t in tops], axis=0)
        total = jnp.zeros((rows, piece), jnp.float32)
        for start in range(0, key_total, piece):
            weights = jnp.exp(score_ref[:, start : start + piece] - top)
            total = total + weights
            weight_ref[head, :, start : start + piece] = weights.astype(jnp.bfloat16)
        inverse = 1.0 / jnp.sum(total, axis=1, keepdims=True)
        inverse_ref[head] = jnp.broadcast_to(inverse, (rows, LANES))
        mixed = dot(weight_ref[head], v_ref[...]) * inverse
        out = jnp.where(head_lanes(out.shape, head, head_size), mixed, out)
    out_ref[...] = out.astype(jnp.bfloat16)


def attention_forward(queries, key_values, head_size, tiles=None, places=None):
    rows, width = queries.shape
    key_total = key_values.shape[0]
    pairs = width // LANES
    group = LANES // head_size
    column = lambda shift: (lambda g, *_: (0, g + shift))
    in_specs = [
        pl.BlockSpec((rows, LANES), column(0)),
        pl.BlockSpec((key_total, LANES), column(0)),
        pl.BlockSpec((key_total, LANES), column(pairs)),
    ]
    operands = [queries, key_values, key_values]
    if tiles is not None:
        in_specs.append(
            pl.BlockSpec((group,) + tiles.shape[1:], lambda g, *_: (g, 0, 0, 0))
        )
        operands.append(tiles)
    grid_spec = pltpu.PrefetchScalarGridSpec(
        num_scalar_prefetch=0 if tiles is None else 1,
        grid=(pairs,),
        in_specs=in_specs,
        out_specs=[
            pl.BlockSpec((rows, LANES), column(0)),
            pl.BlockSpec((group, rows, key_total), lambda g, *_: (g, 0, 0)),
            pl.BlockSpec((group, rows, LANES), lambda g, *_: (g, 0, 0)),
        ],
        scratch_shapes=[pltpu.VMEM((rows, key_total), jnp.float32)],
    )
    heads = width // head_size
    return pl.pallas_call(
        functools.partial(forward_kernel, head_size, tiles is not None),
        grid_spec=grid_spec,
        out_shape=[
            jax.ShapeDtypeStruct((rows, width), jnp.bfloat16),
            jax.ShapeDtypeStruct((heads, rows, key_total), jnp.bfloat16),
            jax.ShapeDtypeStruct((heads, rows, LANES), jnp.float32),
        ],
        compiler_params=pltpu.CompilerParams(vmem_limit_bytes=VMEM_BYTES),
        cost_estimate=pl.CostEstimate(flops=1, bytes_accessed=1, transcendentals=0),
        name="attention_forward",
    )(*(() if places is None else (places,)), *operands)


def backward_kernel(head_size, biased, *refs):
    if biased:
        (q_ref, k_ref, v_ref, grad_ref, out_ref, weight_ref, inverse_ref,
         dq_ref, dkv_ref, dist_ref, ds_ref) = refs
    else:
        (q_ref, k_ref, v_ref, grad_ref, out_ref, weight_ref, inverse_ref,
         dq_ref, dkv_ref, ds_ref) = refs
    rows, key_total = q_ref.shape[0], k_ref.shape[0]
    group = q_ref.shape[1] // head_size
    piece = LANES
    wide = 512
    dq = jnp.zeros(q_ref.shape, jnp.float32)
    grads = grad_ref[...].astype(jnp.float32)
    deltas = grads * out_ref[...].astype(jnp.float32)
    scaled_all = []
    for head in range(group):
        inverse = inverse_ref[head]
        scaled = only_head((grads * inverse).astype(jnp.bfloat16), head, head_size)
        scaled_all.append(scaled)
        delta = jnp.sum(only_head(deltas, head, head_size), axis=1, keepdims=True) * inverse
        for start in range(0, key_total, wide):
            grad_probs = dot_t(scaled, v_ref[start : start + wide, :])
            for half in range(rows // piece):
                for part in range(wide // piece):
                    lo = half * piece
                    at = start + part * piece
                    block = grad_probs[lo : lo + piece, part * piece : (part + 1) * piece]
                    weights = weight_ref[head, lo : lo + piece, at : at + piece]
                    change = weights.astype(jnp.float32) * (block - delta[lo : lo + piece])
                    ds_ref[head * rows + lo : head * rows + lo + piece, at : at + piece] = (
                        change.astype(jnp.bfloat16)
                    )
        mixed = dot(ds_ref[head * rows : (head + 1) * rows, :], k_ref[...])
        dq = jnp.where(head_lanes(dq.shape, head, head_size), mixed, dq)
    dq_ref[...] = dq.astype(jnp.bfloat16)
    queries = jnp.concatenate(
        [only_head(q_ref[...], head, head_size) for head in range(group)], axis=0
    )
    scaled_rows = jnp.concatenate(scaled_all, axis=0)
    for start in range(0, key_total, wide):
        dkv_ref[0, start : start + wide, :] = t_dot(
            ds_ref[:, start : start + wide], queries
        ).astype(jnp.bfloat16)
        weights = jnp.concatenate(
            [weight_ref[head, :, start : start + wide] for head in range(group)], axis=0
        )
        dkv_ref[1, start : start + wide, :] = t_dot(weights, scaled_rows).astype(
            jnp.bfloat16
        )
    if biased:
        down = lax.broadcasted_iota(jnp.int32, (piece, piece), 0)
        across = lax.broadcasted_iota(jnp.int32, (piece, piece), 1)
        flip = (down + across == piece - 1).astype(jnp.bfloat16)
        for head in range(group):
            for half in range(rows // piece):
                lo = head * rows + half * piece
                for start in range(0, key_total, wide):
                    turned = dot(flip, ds_ref[lo : lo + piece, start : start + wide])
                    for part in range(wide // piece):
                        block = turned[:, part * piece : (part + 1) * piece]
                        rolled = pltpu.roll(block, 1, 1, stride=1, stride_axis=0)
                        later = jnp.sum(
                            jnp.where(across <= down, rolled, 0.0), axis=0, keepdims=True
                        )
                        every = jnp.sum(rolled, axis=0, keepdims=True)
                        at = half * (key_total // piece) + start // piece + part
                        dist_ref[head, at : at + 1, :piece] = later
                        dist_ref[head, at : at + 1, piece:] = every - later


def attention_backward(
    queries, key_values, grads, outs, weights, inverses, head_size, biased, first=0, count=None
):
    rows, width = queries.shape
    key_total = key_values.shape[0]
    pairs = width // LANES
    count = pairs if count is None else count
    group = LANES // head_size
    column = lambda shift: (lambda g: (0, g + shift))
    head_block = lambda g: (g + first, 0, 0)
    row_block = pl.BlockSpec((rows, LANES), column(first))
    blocks = rows // LANES * (key_total // LANES)
    out_specs = [
        pl.BlockSpec((rows, LANES), column(0)),
        pl.BlockSpec((2, key_total, LANES), lambda g: (0, 0, g)),
    ]
    out_shape = [
        jax.ShapeDtypeStruct((rows, count * LANES), jnp.bfloat16),
        jax.ShapeDtypeStruct((2, key_total, count * LANES), jnp.bfloat16),
    ]
    if biased:
        out_specs.append(pl.BlockSpec((group, blocks, 2 * LANES), lambda g: (g, 0, 0)))
        out_shape.append(
            jax.ShapeDtypeStruct((group * count, blocks, 2 * LANES), jnp.float32)
        )
    return pl.pallas_call(
        functools.partial(backward_kernel, head_size, biased),
        grid=(count,),
        in_specs=[
            row_block,
            pl.BlockSpec((key_total, LANES), column(first)),
            pl.BlockSpec((key_total, LANES), column(first + pairs)),
            row_block,
            row_block,
            pl.BlockSpec((group, rows, key_total), head_block),
            pl.BlockSpec((group, rows, LANES), head_block),
        ],
        out_specs=out_specs,
        out_shape=out_shape,
        scratch_shapes=[pltpu.VMEM((group * rows, key_total), jnp.bfloat16)],
        compiler_params=pltpu.CompilerParams(vmem_limit_bytes=VMEM_BYTES),
        cost_estimate=pl.CostEstimate(flops=1, bytes_accessed=1, transcendentals=0),
        name="attention_backward",
    )(queries, key_values, key_values, grads, outs, weights, inverses)


def place_kernel(count, at_ref, *refs):
    pieces, whole_ref, held_ref, in_sems, out_sems = refs[:count], *refs[count:]
    rows = held_ref.shape[1]
    parts = in_sems.shape[1]
    width = held_ref.shape[2] // parts
    loads, stores = [], []
    for index in range(count):
        start = pl.multiple_of(at_ref[index] * rows, rows)
        for part in range(parts):
            columns = pl.ds(part * width, width)
            held = held_ref.at[index, :, columns]
            loads.append(
                pltpu.make_async_copy(
                    pieces[index].at[:, columns], held, in_sems.at[index, part]
                )
            )
            stores.append(
                pltpu.make_async_copy(
                    held, whole_ref.at[pl.ds(start, rows), columns], out_sems.at[index, part]
                )
            )
    for load in loads:
        load.start()
    for load, store in zip(loads, stores):
        load.wait()
        store.start()
    for store in stores:
        store.wait()


def place_rows(pieces, places):
    rows, width = pieces[0].shape
    count = len(pieces)
    parts = width // 1024
    return pl.pallas_call(
        functools.partial(place_kernel, count),
        grid_spec=pltpu.PrefetchScalarGridSpec(
            num_scalar_prefetch=1,
            grid=(1,),
            in_specs=[pl.BlockSpec(memory_space=pl.ANY)] * count,
            out_specs=pl.BlockSpec(memory_space=pl.ANY),
            scratch_shapes=[
                pltpu.VMEM((count, rows, width), pieces[0].dtype),
                pltpu.SemaphoreType.DMA((count, parts)),
                pltpu.SemaphoreType.DMA((count, parts)),
            ],
        ),
        out_shape=jax.ShapeDtypeStruct((rows * count, width), pieces[0].dtype),
        compiler_params=pltpu.CompilerParams(vmem_limit_bytes=VMEM_BYTES),
        name="place_rows",
    )(jnp.stack(places).astype(jnp.int32), *pieces)


class Part:
    def __init__(self, array, chosen=()):
        self.array = array
        self.chosen = chosen

    def take(self, bit):
        return Part(self.array, (bit,) + self.chosen)

    def lead(self):
        return (2,) * (self.array.ndim - 2 - len(self.chosen))

    def rows(self):
        return math.prod(self.lead()) * self.array.shape[-2]

    def block(self, width):
        return self.lead() + (1,) * len(self.chosen) + (self.array.shape[-2], width)

    def start(self, places, first):
        whole = len(self.lead())
        return (0,) * whole + tuple(places[first + i] for i in range(len(self.chosen)))


def products_kernel(spans, place_ref, *refs):
    count = len(spans)
    lefts, rights, adds, out_ref = refs[:count], refs[count : 2 * count], refs[2 * count : -1], refs[-1]
    flat = lambda values: values.reshape(-1, values.shape[-1])
    step = pl.program_id(0)
    for index, (first, last) in enumerate(spans):

        @pl.when((step >= first) & (step < last))
        def _(index=index):
            total = dot(flat(lefts[index][...]), rights[index][...])
            for add in adds:
                total = total + flat(add[...]).astype(jnp.float32)
            out_ref[...] = total.astype(jnp.bfloat16)


def products(lefts, rights, adds):
    rows = lefts[0].rows()
    widths = [right.shape[1] for right in rights]
    tile = math.gcd(*widths)
    while tile > 1024:
        tile //= 2
    spans, first = [], 0
    for width in widths:
        spans.append((first, first + width // tile))
        first += width // tile
    places, starts = [jnp.int32(0)], []
    for part in lefts + adds:
        starts.append(len(places))
        places += list(part.chosen)

    def left_spec(part, at):
        return pl.BlockSpec(
            part.block(part.array.shape[-1]),
            lambda step, place_ref: part.start(place_ref, at) + (0, 0),
        )

    def add_spec(part, at):
        return pl.BlockSpec(
            part.block(tile), lambda step, place_ref: part.start(place_ref, at) + (0, step)
        )

    def right_spec(right, span):
        lo, hi = span
        return pl.BlockSpec(
            (right.shape[0], tile),
            lambda step, place_ref: (0, jnp.clip(step - lo, 0, hi - lo - 1)),
        )

    count = len(lefts)
    total = pl.pallas_call(
        functools.partial(products_kernel, spans),
        grid_spec=pltpu.PrefetchScalarGridSpec(
            num_scalar_prefetch=1,
            grid=(first,),
            in_specs=[left_spec(part, at) for part, at in zip(lefts, starts[:count])]
            + [right_spec(right, span) for right, span in zip(rights, spans)]
            + [add_spec(part, at) for part, at in zip(adds, starts[count:])],
            out_specs=pl.BlockSpec((rows, tile), lambda step, place_ref: (0, step)),
        ),
        out_shape=jax.ShapeDtypeStruct((rows, sum(widths)), jnp.bfloat16),
        compiler_params=pltpu.CompilerParams(vmem_limit_bytes=VMEM_BYTES),
        cost_estimate=pl.CostEstimate(flops=1, bytes_accessed=1, transcendentals=0),
        name="products",
    )(
        jnp.stack([jnp.asarray(place, jnp.int32) for place in places]),
        *[part.array for part in lefts],
        *rights,
        *[part.array for part in adds],
    )
    return total.reshape(lefts[0].lead() + (-1, total.shape[1]))


def back_kernel(grad_ref, key_weight_ref, value_weight_ref, out_ref):
    total = dot_t(grad_ref[0], key_weight_ref[...]) + dot_t(grad_ref[1], value_weight_ref[...])
    out_ref[...] = total.astype(jnp.bfloat16)


def back_to_rows(grads, weights, width):
    rows = grads.shape[1]
    tile = math.gcd(rows, 512)
    return pl.pallas_call(
        back_kernel,
        grid=(rows // tile,),
        in_specs=[
            pl.BlockSpec((2, tile, width), lambda step: (0, step, 0)),
            pl.BlockSpec((width, width), lambda step: (0, 1)),
            pl.BlockSpec((width, width), lambda step: (0, 2)),
        ],
        out_specs=pl.BlockSpec((tile, width), lambda step: (step, 0)),
        out_shape=jax.ShapeDtypeStruct((rows, width), jnp.bfloat16),
        compiler_params=pltpu.CompilerParams(vmem_limit_bytes=VMEM_BYTES),
        cost_estimate=pl.CostEstimate(flops=1, bytes_accessed=1, transcendentals=0),
        name="back_to_rows",
    )(grads, weights, weights)


EPSILON = 1e-06


def row_norm(values, gain):
    return values * lax.rsqrt(jnp.mean(values * values, axis=-1, keepdims=True) + EPSILON) * gain


def gated_gelu(gate_up):
    hidden_units = gate_up.shape[1] // 2
    return jax.nn.gelu(gate_up[:, :hidden_units], approximate=True) * gate_up[:, hidden_units:]


def rounded(values):
    return values.astype(jnp.bfloat16)


def distance_rows(by_distance, block):
    heads = by_distance.shape[0]
    padded = jnp.concatenate(
        [
            jnp.full((heads, block - 1), NEGATIVE, jnp.float32),
            by_distance,
            jnp.full((heads, 1), NEGATIVE, jnp.float32),
        ],
        axis=1,
    )
    pieces = padded.reshape(heads, -1, block)[:, :, ::-1]
    rows = jnp.concatenate([pieces[:, :-1], pieces[:, 1:]], axis=2)
    return jnp.concatenate([rows, jnp.full((heads, 1, 2 * block), NEGATIVE, jnp.float32)], axis=1)


def by_distance_sums(rows, block):
    heads, steps, _ = rows.shape
    zero = jnp.zeros((heads, 1, block), jnp.float32)
    pieces = jnp.concatenate([rows[:, :, :block], zero], axis=1) + jnp.concatenate(
        [zero, rows[:, :, block:]], axis=1
    )
    return pieces[:, :, ::-1].reshape(heads, -1)[:, block - 1 : block - 1 + steps * block]


def bit_count(axis_name):
    return int(math.log2(lax.axis_size(axis_name)))


def swap(values, axis_name, bit):
    size = lax.axis_size(axis_name)
    return lax.ppermute(values, axis_name, [(i, i ^ (1 << bit)) for i in range(size)])


def own_bit(axis_name, bit):
    return (lax.axis_index(axis_name) >> bit) & 1


def pick(values, index, axis):
    return lax.dynamic_index_in_dim(values, index, axis, keepdims=False)


def after(value, *others):
    return lax.optimization_barrier((value,) + others)[0]


def far_rows(share):
    held = [(share, lax.axis_index("fsdp"))]
    for bit in reversed(range(1, bit_count("fsdp"))):
        held = held + [(swap(piece, "fsdp", bit), at ^ (1 << bit)) for piece, at in held]
    return held


def near_rows(held):
    return held + [(swap(piece, "fsdp", 0), at ^ 1) for piece, at in held]


def whole_rows(held):
    held = near_rows(held)
    return place_rows([piece for piece, _ in held], [at for _, at in held])


class Product:
    def __init__(self, left, right, parts):
        bits = int(math.log2(parts))
        self.left = Part(
            jnp.transpose(left).reshape(
                (2,) * bits + (left.shape[1] // parts, left.shape[0])
            )
        )
        self.right = right

    def take(self, bit):
        part = Product.__new__(Product)
        part.left = self.left.take(bit)
        part.right = self.right
        return part


class Ready:
    def __init__(self, values, parts):
        bits = int(math.log2(parts))
        self.values = values.reshape(
            (2,) * bits + (values.shape[0] // parts, values.shape[1])
        )

    def take(self, bit):
        part = Ready.__new__(Ready)
        part.values = pick(self.values, bit, self.values.ndim - 3)
        return part

    def value(self):
        return self.values


def joined(own, other, mine):
    return jnp.where(
        mine == 0, jnp.stack([own, other], axis=-3), jnp.stack([other, own], axis=-3)
    )


class Reduction:
    def __init__(self, terms, *stages):
        self.terms = terms
        self.received = []
        self.kept = None
        self.pending = None
        self.gathered = None
        self.plan = []
        for stage in stages:
            bits = [(stage, bit) for bit in range(bit_count("fsdp" if stage == "fsdp" else "ctx"))]
            self.plan += reversed(bits) if stage == "gather" else bits

    def shard(self):
        return self.added(self.terms, self.received)

    def added(self, terms, received):
        if isinstance(terms[0], Ready):
            return terms[0].value()
        return products(
            [term.left for term in terms], [term.right for term in terms], received
        )

    def merged(self):
        if self.gathered is not None:
            own, bit = self.gathered
            return joined(own, self.pending, own_bit("ctx", bit))
        if self.kept is not None:
            return rounded(self.kept.astype(jnp.float32) + self.pending.astype(jnp.float32))
        total = self.shard()
        parts = lax.axis_size("ctx")
        return total.reshape(
            (2,) * bit_count("ctx") + (total.shape[0] // parts, total.shape[1])
        )

    def settle(self, main):
        main = tuple(main)
        if self.pending is not None:
            self.pending, *main = lax.optimization_barrier((self.pending,) + main)
        elif self.received:
            arrays = tuple(part.array for part in self.received)
            arrays, main = lax.optimization_barrier((arrays, main))
            self.received = [
                Part(array, part.chosen) for array, part in zip(arrays, self.received)
            ]
        return tuple(main)

    def prepare(self):
        kind, bit = self.step = self.plan.pop(0)
        if kind == "gather":
            total = self.merged()
            self.gathered = (total, bit)
            return total
        mine = own_bit(kind, bit)
        if kind == "ctx":
            total = self.merged()
            self.kept = pick(total, mine, total.ndim - 3)
            return pick(total, 1 - mine, total.ndim - 3)
        send = self.added(
            [term.take(1 - mine) for term in self.terms],
            [item.take(1 - mine) for item in self.received],
        )
        self.terms = [term.take(mine) for term in self.terms]
        self.received = [item.take(mine) for item in self.received]
        return send

    def exchange(self, send):
        kind, bit = self.step
        other = swap(send, "fsdp" if kind == "fsdp" else "ctx", bit)
        if kind == "fsdp":
            self.received.append(Part(other))
        else:
            self.pending = other

    def result(self):
        total = self.merged()
        return total.reshape(-1, total.shape[-1])


class Gathering(Reduction):
    def __init__(self, rows):
        super().__init__([Ready(rows, 1)], "gather")

    def merged(self):
        return super().merged() if self.gathered is not None else self.shard()


def finish(item):
    while item.plan:
        advance([item])
    return item.shard()


def advance(sums, *main):
    if main:
        for item in sums:
            main = item.settle(main)
    sends = [item.prepare() for item in sums]
    held = lax.optimization_barrier(tuple(sends) + tuple(main))
    for item, send in zip(sums, held):
        item.exchange(send)
    main = held[len(sums) :]
    return main[0] if len(main) == 1 else main


def weighed(weight, grad):
    return jnp.sum(weight.astype(jnp.float32) * grad[:, : weight.shape[1]], axis=1)


def body(tokens, encoded, cotangent, w_self, w_cross, w_ffn, gains, table, bucket_ids, block_order):
    row_count = tokens.shape[1]
    model_width = tokens.shape[2]
    head_count = table.shape[1]
    head_size = model_width // head_count
    hidden_units = w_ffn.shape[1] // 3
    block = row_count // 2
    seq_length = bucket_ids.shape[0]
    steps = seq_length // block
    ctx_place = lax.axis_index("ctx")
    fsdp_size = lax.axis_size("fsdp")
    small = jnp.concatenate([gains.reshape(1, -1), table.reshape(1, -1)], axis=1)
    far_small = far_rows(small)
    held_self = far_rows(w_self)
    held_self = near_rows(
        [(after(piece, *[other for other, _ in far_small[1:]]), at) for piece, at in held_self]
    )
    small_held = near_rows(far_small)
    small = jnp.zeros((fsdp_size, small.shape[1]), small.dtype)
    for piece, at in small_held:
        small = lax.dynamic_update_slice_in_dim(small, piece, at, 0)
    gain_rows = jnp.transpose(
        small[:, : gains.size].reshape((fsdp_size,) + gains.shape), (1, 0, 2)
    ).reshape(gains.shape[0], -1)
    table_rows = small[:, gains.size :].reshape(-1, head_count)
    token_rows = lax.all_gather(tokens[0], "ctx", axis=0, tiled=True)
    encoder_sum = Gathering(encoded[0])
    advance([encoder_sum])
    held_cross = far_rows(after(w_cross, small, *[piece for piece, _ in held_self[1:]]))
    held_ffn = far_rows(after(w_ffn, *[piece for piece, _ in held_cross[1:]]))
    whole_self = place_rows([piece for piece, _ in held_self], [at for _, at in held_self])
    encoder_sum.pending = after(encoder_sum.pending, whole_self[:8, :LANES])
    advance([encoder_sum])
    gain_float = gain_rows.astype(jnp.float32)
    bucket_count = table_rows.shape[0]
    in_bucket = (
        bucket_ids[None, :] == jnp.arange(bucket_count, dtype=jnp.int32)[:, None]
    ).astype(jnp.float32)
    by_distance = lax.dot_general(
        table_rows.astype(jnp.float32),
        in_bucket,
        (((0,), (0,)), ((), ())),
        precision=lax.Precision.HIGHEST,
    )
    tiles = bias_tiles(
        after(distance_rows(by_distance, block), whole_self), LANES // head_size
    )
    own_blocks = lax.dynamic_slice_in_dim(block_order, 2 * ctx_place, 2)
    apart = own_blocks[:, None] - block_order[None, :]
    places = jnp.where(apart < 0, steps, apart).astype(jnp.int32).reshape(-1)

    inputs = tokens[0].astype(jnp.float32)
    gain_first = after(gain_float[0], tiles)
    normed_all = rounded(row_norm(token_rows.astype(jnp.float32), gain_first))
    normed_all = advance([encoder_sum], normed_all)
    normed_one = rounded(row_norm(inputs, gain_float[0]))
    queries = rounded(dot(normed_one, whole_self[:, :model_width]))
    key_values = rounded(dot(normed_all, whole_self[:, model_width : 3 * model_width]))
    held_cross = near_rows([(after(piece, normed_one), at) for piece, at in held_cross])
    attended, weights, inverses = attention_forward(queries, key_values, head_size, tiles, places)
    held_cross = [(after(piece, attended), at) for piece, at in held_cross]
    whole_cross = place_rows([piece for piece, _ in held_cross], [at for _, at in held_cross])
    after_one = inputs + dot(attended, whole_self[:, 3 * model_width :])
    normed_two = rounded(row_norm(after_one, gain_float[1]))
    cross_query = rounded(dot(normed_two, whole_cross[:, :model_width]))
    cross_query = encoder_sum.settle((cross_query,))[0]
    while encoder_sum.plan:
        cross_query = advance([encoder_sum], cross_query)
    encoder_all = encoder_sum.result()
    encoder_kv = rounded(dot(encoder_all, whole_cross[:, model_width : 3 * model_width]))
    held_ffn = near_rows([(after(piece, encoder_kv), at) for piece, at in held_ffn])
    cross_rows, cross_weights, cross_inverses = attention_forward(
        cross_query, encoder_kv, head_size
    )
    held_ffn = [(after(piece, cross_rows), at) for piece, at in held_ffn]
    whole_ffn = place_rows([piece for piece, _ in held_ffn], [at for _, at in held_ffn])
    after_two = after_one + dot(cross_rows, whole_cross[:, 3 * model_width :])
    normed_three = rounded(row_norm(after_two, gain_float[2]))
    gate_up = dot(normed_three, whole_ffn[:, : 2 * hidden_units])
    mixed_float, gated_back = jax.vjp(gated_gelu, gate_up)
    mixed_rows = rounded(mixed_float)
    output = rounded(after_two + dot_t(mixed_rows, whole_ffn[:, 2 * hidden_units :]))

    grad_branch_three = cotangent[0]
    grad_after_two = grad_branch_three.astype(jnp.float32)
    grad_mixed = dot(grad_branch_three, whole_ffn[:, 2 * hidden_units :])
    grad_gate_up = rounded(gated_back(grad_mixed)[0])
    grad_normed_three = dot_t(grad_gate_up, whole_ffn[:, : 2 * hidden_units])
    ffn_sum = Reduction(
        [
            Product(normed_three, grad_gate_up, fsdp_size),
            Product(grad_branch_three, mixed_rows, fsdp_size),
        ],
        "fsdp",
    )
    grad_normed_three = advance([ffn_sum], grad_normed_three)
    norm_part = jax.vjp(row_norm, after_two, gain_float[2])[1](grad_normed_three)[0]
    grad_after_one = grad_after_two + norm_part
    grad_branch_two = rounded(grad_after_one)
    grad_cross_rows = rounded(dot_t(grad_branch_two, whole_cross[:, 3 * model_width :]))
    grad_cross_rows = advance([ffn_sum], grad_cross_rows)
    grad_cross_query, encoder_full = attention_backward(
        cross_query, encoder_kv, grad_cross_rows, cross_rows, cross_weights, cross_inverses,
        head_size, False,
    )
    grad_normed_two = dot_t(grad_cross_query, whole_cross[:, :model_width])
    norm_part = jax.vjp(row_norm, after_one, gain_float[1])[1](grad_normed_two)[0]
    grad_inputs_one = grad_after_one + norm_part
    grad_branch_one = rounded(grad_inputs_one)
    grad_attended = rounded(dot_t(grad_branch_one, whole_self[:, 3 * model_width :]))
    cross_sum = Reduction(
        [
            Product(normed_two, grad_cross_query, fsdp_size),
            Product(encoder_all, encoder_full[0], fsdp_size),
            Product(encoder_all, encoder_full[1], fsdp_size),
            Product(cross_rows, grad_branch_two, fsdp_size),
        ],
        "fsdp",
    )
    grad_encoder_part = back_to_rows(encoder_full, whole_cross, model_width)
    encoder_back = Reduction([Ready(grad_encoder_part, 1)], "ctx")
    grad_attended = advance([cross_sum, encoder_back], grad_attended)
    grad_query, grad_keys, distance_sums = attention_backward(
        queries, key_values, grad_attended, attended, weights, inverses, head_size, True
    )
    self_sum = Reduction(
        [
            Product(normed_one, grad_query, fsdp_size),
            Product(normed_all, grad_keys[0], fsdp_size),
            Product(normed_all, grad_keys[1], fsdp_size),
            Product(attended, grad_branch_one, fsdp_size),
        ],
        "fsdp",
    )
    grad_query, grad_keys, distance_sums = advance(
        [self_sum], grad_query, grad_keys, distance_sums
    )
    ffn_shard, grad_query, grad_keys, distance_sums = lax.optimization_barrier(
        (finish(ffn_sum), grad_query, grad_keys, distance_sums)
    )
    grad_query, grad_keys = advance([cross_sum], grad_query, grad_keys)
    ffn_shard = lax.psum_scatter(ffn_shard, "ctx", scatter_dimension=0, tiled=True)
    key_weights = whole_self[:, model_width : 2 * model_width]
    value_weights = whole_self[:, 2 * model_width : 3 * model_width]
    grad_normed_part = back_to_rows(grad_keys, whole_self, model_width)
    token_sum = Reduction([Ready(grad_normed_part, 1)], "ctx")
    distance_sums = advance([token_sum], distance_sums)
    distance_sums = advance([self_sum], distance_sums)
    distance_sums = cross_sum.settle((distance_sums,))[0]
    distance_sums = advance([encoder_back], distance_sums)
    in_place = (places[None, :] == jnp.arange(steps, dtype=jnp.int32)[:, None]).astype(jnp.float32)
    distance_sums = jnp.einsum(
        "sp,hpw->hsw", in_place, distance_sums, precision=lax.Precision.HIGHEST
    )
    grad_table = lax.dot_general(
        in_bucket,
        by_distance_sums(distance_sums, block),
        (((1,), (1,)), ((), ())),
        precision=lax.Precision.HIGHEST,
    )
    grad_normed_query = dot_t(grad_query, whole_self[:, :model_width])
    cross_rest = Reduction([Ready(finish(cross_sum), 1)], "ctx", "gather")
    grad_table = advance([cross_rest], grad_table)
    for bit in range(bit_count("fsdp")):
        grad_table = grad_table + swap(grad_table, "fsdp", bit)
    table_columns = jnp.pad(
        lax.dynamic_slice_in_dim(
            grad_table, lax.axis_index("fsdp") * table.shape[0], table.shape[0], 0
        ),
        ((0, gains.shape[1] - table.shape[0]), (0, LANES - head_count)),
    )
    rest = jnp.concatenate([finish(self_sum), rounded(table_columns)], axis=1)
    rest = advance([token_sum, encoder_back], rest)
    ffn_shard, rest = lax.optimization_barrier((ffn_shard, rest))
    ffn_rows = lax.all_gather(ffn_shard, "ctx", axis=0, tiled=True)
    rest_sum = Reduction([Ready(rest, 1)], "ctx", "gather")
    advance([rest_sum])
    advance([cross_rest])
    ahead = [token_sum, encoder_back, cross_rest]
    while rest_sum.plan:
        ahead = [item for item in ahead if item.plan]
        if ahead:
            rest_sum.pending = advance(ahead, rest_sum.pending)
        if len(rest_sum.plan) == bit_count("ctx"):
            rest_sum.pending, ffn_rows = lax.optimization_barrier((rest_sum.pending, ffn_rows))
        advance([rest_sum])
    while any(item.plan for item in ahead):
        advance([item for item in ahead if item.plan])
    grad_normed_one = grad_normed_query + token_sum.result().astype(jnp.float32)
    norm_part = jax.vjp(row_norm, inputs, gain_float[0])[1](grad_normed_one)[0]
    grad_tokens = rounded(grad_inputs_one + norm_part)
    grad_encoded = encoder_back.result()
    ffn_grad = ffn_rows.astype(jnp.float32)
    cross_grad = cross_rest.result().astype(jnp.float32)
    rest = rest_sum.result().astype(jnp.float32)
    self_grad = rest[:, : 4 * model_width]
    table_own = rest[: table.shape[0], 4 * model_width : 4 * model_width + head_count]
    gain_own = jnp.stack(
        [
            weighed(w_self[:, : 3 * model_width], self_grad),
            weighed(w_cross[:, :model_width], cross_grad),
            weighed(w_ffn[:, : 2 * hidden_units], ffn_grad),
        ]
    ) / gains.astype(jnp.float32)
    return (
        output[None],
        grad_tokens[None],
        grad_encoded[None],
        self_grad,
        cross_grad,
        ffn_grad,
        gain_own,
        table_own,
    )


def solution(mesh):
    in_specs = (
        P("fsdp", "ctx", None),
        P("fsdp", "ctx", None),
        P("fsdp", "ctx", None),
        P("fsdp", None),
        P("fsdp", None),
        P("fsdp", None),
        P(None, "fsdp"),
        P("fsdp", None),
        P(),
        P(),
    )
    out_specs = (
        P("fsdp", "ctx", None),
        P("fsdp", "ctx", None),
        P("fsdp", "ctx", None),
        P("fsdp", None),
        P("fsdp", None),
        P("fsdp", None),
        P(None, "fsdp"),
        P("fsdp", None),
    )
    return jax.shard_map(body, mesh=mesh, in_specs=in_specs, out_specs=out_specs, check_vma=False)
```

```python
import functools
import math

import jax
import jax.numpy as jnp
from jax import lax
from jax.experimental import pallas as pl
from jax.experimental.pallas import tpu as pltpu
from jax.sharding import PartitionSpec as P

NEGATIVE = -1e30
LANES = 128
VMEM_BYTES = 56 * 2**20


def dot(left, right):
    return lax.dot_general(
        left, right, (((1,), (0,)), ((), ())), preferred_element_type=jnp.float32
    )


def dot_t(left, right):
    return lax.dot_general(
        left, right, (((1,), (1,)), ((), ())), preferred_element_type=jnp.float32
    )


def t_dot(left, right):
    return lax.dot_general(
        left, right, (((0,), (0,)), ((), ())), preferred_element_type=jnp.float32
    )


def head_lanes(shape, head, head_size):
    lane = lax.broadcasted_iota(jnp.int32, shape, len(shape) - 1)
    return (lane >= head * head_size) & (lane < (head + 1) * head_size)


def only_head(values, head, head_size):
    return jnp.where(head_lanes(values.shape, head, head_size), values, jnp.zeros_like(values))


def tile_kernel(vector_ref, tile_ref):
    size = tile_ref.shape[-1]
    for head in range(vector_ref.shape[0]):
        for step in range(vector_ref.shape[1]):
            row = jnp.broadcast_to(
                vector_ref[head, step : step + 1, :], (size, 2 * size)
            )
            rolled = pltpu.roll(row, 0, 1, stride=1, stride_axis=0)
            tile_ref[head, step] = rolled[:, :size].astype(jnp.bfloat16)


def bias_tiles(vectors, group):
    head_count, steps, width = vectors.shape
    size = width // 2
    return pl.pallas_call(
        tile_kernel,
        grid=(head_count // group,),
        in_specs=[pl.BlockSpec((group, steps, width), lambda g: (g, 0, 0))],
        out_specs=pl.BlockSpec((group, steps, size, size), lambda g: (g, 0, 0, 0)),
        out_shape=jax.ShapeDtypeStruct((head_count, steps, size, size), jnp.bfloat16),
        compiler_params=pltpu.CompilerParams(vmem_limit_bytes=VMEM_BYTES),
        name="bias_tiles",
    )(vectors)


def forward_kernel(head_size, biased, *refs):
    if biased:
        place_ref, q_ref, k_ref, v_ref, tile_ref, out_ref, weight_ref, inverse_ref, score_ref = refs
    else:
        q_ref, k_ref, v_ref, out_ref, weight_ref, inverse_ref, score_ref = refs
    rows, key_total = q_ref.shape[0], k_ref.shape[0]
    group = q_ref.shape[1] // head_size
    piece = LANES
    out = jnp.zeros(q_ref.shape, jnp.float32)
    for head in range(group):
        query = only_head(q_ref[...], head, head_size)
        tops = [None] * (rows // piece)
        wide = 512
        for start in range(0, key_total, wide):
            scores = dot_t(query, k_ref[start : start + wide, :])
            for half in range(rows // piece):
                for part in range(wide // piece):
                    block = scores[
                        half * piece : (half + 1) * piece, part * piece : (part + 1) * piece
                    ]
                    key_block = start // piece + part
                    if biased:
                        place = place_ref[half * (key_total // piece) + key_block]
                        block = block + tile_ref[head, place].astype(jnp.float32)
                    score_ref[
                        half * piece : (half + 1) * piece,
                        key_block * piece : (key_block + 1) * piece,
                    ] = block
                    tops[half] = block if tops[half] is None else jnp.maximum(tops[half], block)
        top = jnp.concatenate([jnp.max(t, axis=1, keepdims=True) for t in tops], axis=0)
        total = jnp.zeros((rows, piece), jnp.float32)
        for start in range(0, key_total, piece):
            weights = jnp.exp(score_ref[:, start : start + piece] - top)
            total = total + weights
            weight_ref[head, :, start : start + piece] = weights.astype(jnp.bfloat16)
        inverse = 1.0 / jnp.sum(total, axis=1, keepdims=True)
        inverse_ref[head] = jnp.broadcast_to(inverse, (rows, LANES))
        mixed = dot(weight_ref[head], v_ref[...]) * inverse
        out = jnp.where(head_lanes(out.shape, head, head_size), mixed, out)
    out_ref[...] = out.astype(jnp.bfloat16)


def attention_forward(queries, key_values, head_size, tiles=None, places=None):
    rows, width = queries.shape
    key_total = key_values.shape[0]
    pairs = width // LANES
    group = LANES // head_size
    column = lambda shift: (lambda g, *_: (0, g + shift))
    in_specs = [
        pl.BlockSpec((rows, LANES), column(0)),
        pl.BlockSpec((key_total, LANES), column(0)),
        pl.BlockSpec((key_total, LANES), column(pairs)),
    ]
    operands = [queries, key_values, key_values]
    if tiles is not None:
        in_specs.append(
            pl.BlockSpec((group,) + tiles.shape[1:], lambda g, *_: (g, 0, 0, 0))
        )
        operands.append(tiles)
    grid_spec = pltpu.PrefetchScalarGridSpec(
        num_scalar_prefetch=0 if tiles is None else 1,
        grid=(pairs,),
        in_specs=in_specs,
        out_specs=[
            pl.BlockSpec((rows, LANES), column(0)),
            pl.BlockSpec((group, rows, key_total), lambda g, *_: (g, 0, 0)),
            pl.BlockSpec((group, rows, LANES), lambda g, *_: (g, 0, 0)),
        ],
        scratch_shapes=[pltpu.VMEM((rows, key_total), jnp.float32)],
    )
    heads = width // head_size
    return pl.pallas_call(
        functools.partial(forward_kernel, head_size, tiles is not None),
        grid_spec=grid_spec,
        out_shape=[
            jax.ShapeDtypeStruct((rows, width), jnp.bfloat16),
            jax.ShapeDtypeStruct((heads, rows, key_total), jnp.bfloat16),
            jax.ShapeDtypeStruct((heads, rows, LANES), jnp.float32),
        ],
        compiler_params=pltpu.CompilerParams(vmem_limit_bytes=VMEM_BYTES),
        cost_estimate=pl.CostEstimate(flops=1, bytes_accessed=1, transcendentals=0),
        name="attention_forward",
    )(*(() if places is None else (places,)), *operands)


def backward_kernel(head_size, biased, *refs):
    if biased:
        (q_ref, k_ref, v_ref, grad_ref, out_ref, weight_ref, inverse_ref,
         dq_ref, dkv_ref, dist_ref, ds_ref) = refs
    else:
        (q_ref, k_ref, v_ref, grad_ref, out_ref, weight_ref, inverse_ref,
         dq_ref, dkv_ref, ds_ref) = refs
    rows, key_total = q_ref.shape[0], k_ref.shape[0]
    group = q_ref.shape[1] // head_size
    piece = LANES
    wide = 512
    dq = jnp.zeros(q_ref.shape, jnp.float32)
    grads = grad_ref[...].astype(jnp.float32)
    deltas = grads * out_ref[...].astype(jnp.float32)
    scaled_all = []
    for head in range(group):
        inverse = inverse_ref[head]
        scaled = only_head((grads * inverse).astype(jnp.bfloat16), head, head_size)
        scaled_all.append(scaled)
        delta = jnp.sum(only_head(deltas, head, head_size), axis=1, keepdims=True) * inverse
        for start in range(0, key_total, wide):
            grad_probs = dot_t(scaled, v_ref[start : start + wide, :])
            for half in range(rows // piece):
                for part in range(wide // piece):
                    lo = half * piece
                    at = start + part * piece
                    block = grad_probs[lo : lo + piece, part * piece : (part + 1) * piece]
                    weights = weight_ref[head, lo : lo + piece, at : at + piece]
                    change = weights.astype(jnp.float32) * (block - delta[lo : lo + piece])
                    ds_ref[head * rows + lo : head * rows + lo + piece, at : at + piece] = (
                        change.astype(jnp.bfloat16)
                    )
        mixed = dot(ds_ref[head * rows : (head + 1) * rows, :], k_ref[...])
        dq = jnp.where(head_lanes(dq.shape, head, head_size), mixed, dq)
    dq_ref[...] = dq.astype(jnp.bfloat16)
    queries = jnp.concatenate(
        [only_head(q_ref[...], head, head_size) for head in range(group)], axis=0
    )
    scaled_rows = jnp.concatenate(scaled_all, axis=0)
    for start in range(0, key_total, wide):
        dkv_ref[0, start : start + wide, :] = t_dot(
            ds_ref[:, start : start + wide], queries
        ).astype(jnp.bfloat16)
        weights = jnp.concatenate(
            [weight_ref[head, :, start : start + wide] for head in range(group)], axis=0
        )
        dkv_ref[1, start : start + wide, :] = t_dot(weights, scaled_rows).astype(
            jnp.bfloat16
        )
    if biased:
        down = lax.broadcasted_iota(jnp.int32, (piece, piece), 0)
        across = lax.broadcasted_iota(jnp.int32, (piece, piece), 1)
        flip = (down + across == piece - 1).astype(jnp.bfloat16)
        for head in range(group):
            for half in range(rows // piece):
                lo = head * rows + half * piece
                for start in range(0, key_total, wide):
                    turned = dot(flip, ds_ref[lo : lo + piece, start : start + wide])
                    for part in range(wide // piece):
                        block = turned[:, part * piece : (part + 1) * piece]
                        rolled = pltpu.roll(block, 1, 1, stride=1, stride_axis=0)
                        later = jnp.sum(
                            jnp.where(across <= down, rolled, 0.0), axis=0, keepdims=True
                        )
                        every = jnp.sum(rolled, axis=0, keepdims=True)
                        at = half * (key_total // piece) + start // piece + part
                        dist_ref[head, at : at + 1, :piece] = later
                        dist_ref[head, at : at + 1, piece:] = every - later


def attention_backward(
    queries, key_values, grads, outs, weights, inverses, head_size, biased, first=0, count=None
):
    rows, width = queries.shape
    key_total = key_values.shape[0]
    pairs = width // LANES
    count = pairs if count is None else count
    group = LANES // head_size
    column = lambda shift: (lambda g: (0, g + shift))
    head_block = lambda g: (g + first, 0, 0)
    row_block = pl.BlockSpec((rows, LANES), column(first))
    blocks = rows // LANES * (key_total // LANES)
    out_specs = [
        pl.BlockSpec((rows, LANES), column(0)),
        pl.BlockSpec((2, key_total, LANES), lambda g: (0, 0, g)),
    ]
    out_shape = [
        jax.ShapeDtypeStruct((rows, count * LANES), jnp.bfloat16),
        jax.ShapeDtypeStruct((2, key_total, count * LANES), jnp.bfloat16),
    ]
    if biased:
        out_specs.append(pl.BlockSpec((group, blocks, 2 * LANES), lambda g: (g, 0, 0)))
        out_shape.append(
            jax.ShapeDtypeStruct((group * count, blocks, 2 * LANES), jnp.float32)
        )
    return pl.pallas_call(
        functools.partial(backward_kernel, head_size, biased),
        grid=(count,),
        in_specs=[
            row_block,
            pl.BlockSpec((key_total, LANES), column(first)),
            pl.BlockSpec((key_total, LANES), column(first + pairs)),
            row_block,
            row_block,
            pl.BlockSpec((group, rows, key_total), head_block),
            pl.BlockSpec((group, rows, LANES), head_block),
        ],
        out_specs=out_specs,
        out_shape=out_shape,
        scratch_shapes=[pltpu.VMEM((group * rows, key_total), jnp.bfloat16)],
        compiler_params=pltpu.CompilerParams(vmem_limit_bytes=VMEM_BYTES),
        cost_estimate=pl.CostEstimate(flops=1, bytes_accessed=1, transcendentals=0),
        name="attention_backward",
    )(queries, key_values, key_values, grads, outs, weights, inverses)


def place_kernel(count, at_ref, *refs):
    pieces, whole_ref, held_ref, in_sems, out_sems = refs[:count], *refs[count:]
    rows = held_ref.shape[1]
    parts = in_sems.shape[1]
    width = held_ref.shape[2] // parts
    loads, stores = [], []
    for index in range(count):
        start = pl.multiple_of(at_ref[index] * rows, rows)
        for part in range(parts):
            columns = pl.ds(part * width, width)
            held = held_ref.at[index, :, columns]
            loads.append(
                pltpu.make_async_copy(
                    pieces[index].at[:, columns], held, in_sems.at[index, part]
                )
            )
            stores.append(
                pltpu.make_async_copy(
                    held, whole_ref.at[pl.ds(start, rows), columns], out_sems.at[index, part]
                )
            )
    for load in loads:
        load.start()
    for load, store in zip(loads, stores):
        load.wait()
        store.start()
    for store in stores:
        store.wait()


def place_rows(pieces, places):
    rows, width = pieces[0].shape
    count = len(pieces)
    parts = width // 1024
    return pl.pallas_call(
        functools.partial(place_kernel, count),
        grid_spec=pltpu.PrefetchScalarGridSpec(
            num_scalar_prefetch=1,
            grid=(1,),
            in_specs=[pl.BlockSpec(memory_space=pl.ANY)] * count,
            out_specs=pl.BlockSpec(memory_space=pl.ANY),
            scratch_shapes=[
                pltpu.VMEM((count, rows, width), pieces[0].dtype),
                pltpu.SemaphoreType.DMA((count, parts)),
                pltpu.SemaphoreType.DMA((count, parts)),
            ],
        ),
        out_shape=jax.ShapeDtypeStruct((rows * count, width), pieces[0].dtype),
        compiler_params=pltpu.CompilerParams(vmem_limit_bytes=VMEM_BYTES),
        name="place_rows",
    )(jnp.stack(places).astype(jnp.int32), *pieces)


class Part:
    def __init__(self, array, chosen=()):
        self.array = array
        self.chosen = chosen

    def take(self, bit):
        return Part(self.array, (bit,) + self.chosen)

    def lead(self):
        return (2,) * (self.array.ndim - 2 - len(self.chosen))

    def rows(self):
        return math.prod(self.lead()) * self.array.shape[-2]

    def block(self, width):
        return self.lead() + (1,) * len(self.chosen) + (self.array.shape[-2], width)

    def start(self, places, first):
        whole = len(self.lead())
        return (0,) * whole + tuple(places[first + i] for i in range(len(self.chosen)))


def products_kernel(spans, place_ref, *refs):
    count = len(spans)
    lefts, rights, adds, out_ref = refs[:count], refs[count : 2 * count], refs[2 * count : -1], refs[-1]
    flat = lambda values: values.reshape(-1, values.shape[-1])
    step = pl.program_id(0)
    for index, (first, last) in enumerate(spans):

        @pl.when((step >= first) & (step < last))
        def _(index=index):
            total = dot(flat(lefts[index][...]), rights[index][...])
            for add in adds:
                total = total + flat(add[...]).astype(jnp.float32)
            out_ref[...] = total.astype(jnp.bfloat16)


def products(lefts, rights, adds):
    rows = lefts[0].rows()
    widths = [right.shape[1] for right in rights]
    tile = math.gcd(*widths)
    while tile > 1024:
        tile //= 2
    spans, first = [], 0
    for width in widths:
        spans.append((first, first + width // tile))
        first += width // tile
    places, starts = [jnp.int32(0)], []
    for part in lefts + adds:
        starts.append(len(places))
        places += list(part.chosen)

    def left_spec(part, at):
        return pl.BlockSpec(
            part.block(part.array.shape[-1]),
            lambda step, place_ref: part.start(place_ref, at) + (0, 0),
        )

    def add_spec(part, at):
        return pl.BlockSpec(
            part.block(tile), lambda step, place_ref: part.start(place_ref, at) + (0, step)
        )

    def right_spec(right, span):
        lo, hi = span
        return pl.BlockSpec(
            (right.shape[0], tile),
            lambda step, place_ref: (0, jnp.clip(step - lo, 0, hi - lo - 1)),
        )

    count = len(lefts)
    total = pl.pallas_call(
        functools.partial(products_kernel, spans),
        grid_spec=pltpu.PrefetchScalarGridSpec(
            num_scalar_prefetch=1,
            grid=(first,),
            in_specs=[left_spec(part, at) for part, at in zip(lefts, starts[:count])]
            + [right_spec(right, span) for right, span in zip(rights, spans)]
            + [add_spec(part, at) for part, at in zip(adds, starts[count:])],
            out_specs=pl.BlockSpec((rows, tile), lambda step, place_ref: (0, step)),
        ),
        out_shape=jax.ShapeDtypeStruct((rows, sum(widths)), jnp.bfloat16),
        compiler_params=pltpu.CompilerParams(vmem_limit_bytes=VMEM_BYTES),
        cost_estimate=pl.CostEstimate(flops=1, bytes_accessed=1, transcendentals=0),
        name="products",
    )(
        jnp.stack([jnp.asarray(place, jnp.int32) for place in places]),
        *[part.array for part in lefts],
        *rights,
        *[part.array for part in adds],
    )
    return total.reshape(lefts[0].lead() + (-1, total.shape[1]))


def back_kernel(grad_ref, key_weight_ref, value_weight_ref, out_ref):
    total = dot_t(grad_ref[0], key_weight_ref[...]) + dot_t(grad_ref[1], value_weight_ref[...])
    out_ref[...] = total.astype(jnp.bfloat16)


def back_to_rows(grads, weights, width):
    rows = grads.shape[1]
    tile = math.gcd(rows, 512)
    return pl.pallas_call(
        back_kernel,
        grid=(rows // tile,),
        in_specs=[
            pl.BlockSpec((2, tile, width), lambda step: (0, step, 0)),
            pl.BlockSpec((width, width), lambda step: (0, 1)),
            pl.BlockSpec((width, width), lambda step: (0, 2)),
        ],
        out_specs=pl.BlockSpec((tile, width), lambda step: (step, 0)),
        out_shape=jax.ShapeDtypeStruct((rows, width), jnp.bfloat16),
        compiler_params=pltpu.CompilerParams(vmem_limit_bytes=VMEM_BYTES),
        cost_estimate=pl.CostEstimate(flops=1, bytes_accessed=1, transcendentals=0),
        name="back_to_rows",
    )(grads, weights, weights)


EPSILON = 1e-06


def row_norm(values, gain):
    return values * lax.rsqrt(jnp.mean(values * values, axis=-1, keepdims=True) + EPSILON) * gain


def gated_gelu(gate_up):
    hidden_units = gate_up.shape[1] // 2
    return jax.nn.gelu(gate_up[:, :hidden_units], approximate=True) * gate_up[:, hidden_units:]


def rounded(values):
    return values.astype(jnp.bfloat16)


def distance_rows(by_distance, block):
    heads = by_distance.shape[0]
    padded = jnp.concatenate(
        [
            jnp.full((heads, block - 1), NEGATIVE, jnp.float32),
            by_distance,
            jnp.full((heads, 1), NEGATIVE, jnp.float32),
        ],
        axis=1,
    )
    pieces = padded.reshape(heads, -1, block)[:, :, ::-1]
    rows = jnp.concatenate([pieces[:, :-1], pieces[:, 1:]], axis=2)
    return jnp.concatenate([rows, jnp.full((heads, 1, 2 * block), NEGATIVE, jnp.float32)], axis=1)


def by_distance_sums(rows, block):
    heads, steps, _ = rows.shape
    zero = jnp.zeros((heads, 1, block), jnp.float32)
    pieces = jnp.concatenate([rows[:, :, :block], zero], axis=1) + jnp.concatenate(
        [zero, rows[:, :, block:]], axis=1
    )
    return pieces[:, :, ::-1].reshape(heads, -1)[:, block - 1 : block - 1 + steps * block]


def bit_count(axis_name):
    return int(math.log2(lax.axis_size(axis_name)))


def swap(values, axis_name, bit):
    size = lax.axis_size(axis_name)
    return lax.ppermute(values, axis_name, [(i, i ^ (1 << bit)) for i in range(size)])


def own_bit(axis_name, bit):
    return (lax.axis_index(axis_name) >> bit) & 1


def pick(values, index, axis):
    return lax.dynamic_index_in_dim(values, index, axis, keepdims=False)


def after(value, *others):
    return lax.optimization_barrier((value,) + others)[0]


def far_rows(share):
    held = [(share, lax.axis_index("fsdp"))]
    for bit in reversed(range(1, bit_count("fsdp"))):
        held = held + [(swap(piece, "fsdp", bit), at ^ (1 << bit)) for piece, at in held]
    return held


def near_rows(held):
    return held + [(swap(piece, "fsdp", 0), at ^ 1) for piece, at in held]


def whole_rows(held):
    held = near_rows(held)
    return place_rows([piece for piece, _ in held], [at for _, at in held])


class Product:
    def __init__(self, left, right, parts):
        bits = int(math.log2(parts))
        self.left = Part(
            jnp.transpose(left).reshape(
                (2,) * bits + (left.shape[1] // parts, left.shape[0])
            )
        )
        self.right = right

    def take(self, bit):
        part = Product.__new__(Product)
        part.left = self.left.take(bit)
        part.right = self.right
        return part


class Ready:
    def __init__(self, values, parts):
        bits = int(math.log2(parts))
        self.values = values.reshape(
            (2,) * bits + (values.shape[0] // parts, values.shape[1])
        )

    def take(self, bit):
        part = Ready.__new__(Ready)
        part.values = pick(self.values, bit, self.values.ndim - 3)
        return part

    def value(self):
        return self.values


def joined(own, other, mine):
    return jnp.where(
        mine == 0, jnp.stack([own, other], axis=-3), jnp.stack([other, own], axis=-3)
    )


class Reduction:
    def __init__(self, terms, *stages):
        self.terms = terms
        self.received = []
        self.kept = None
        self.pending = None
        self.gathered = None
        self.plan = []
        for stage in stages:
            bits = [(stage, bit) for bit in range(bit_count("fsdp" if stage == "fsdp" else "ctx"))]
            self.plan += reversed(bits) if stage == "gather" else bits

    def shard(self):
        return self.added(self.terms, self.received)

    def added(self, terms, received):
        if isinstance(terms[0], Ready):
            return terms[0].value()
        return products(
            [term.left for term in terms], [term.right for term in terms], received
        )

    def merged(self):
        if self.gathered is not None:
            own, bit = self.gathered
            return joined(own, self.pending, own_bit("ctx", bit))
        if self.kept is not None:
            return rounded(self.kept.astype(jnp.float32) + self.pending.astype(jnp.float32))
        total = self.shard()
        parts = lax.axis_size("ctx")
        return total.reshape(
            (2,) * bit_count("ctx") + (total.shape[0] // parts, total.shape[1])
        )

    def settle(self, main):
        main = tuple(main)
        if self.pending is not None:
            self.pending, *main = lax.optimization_barrier((self.pending,) + main)
        elif self.received:
            arrays = tuple(part.array for part in self.received)
            arrays, main = lax.optimization_barrier((arrays, main))
            self.received = [
                Part(array, part.chosen) for array, part in zip(arrays, self.received)
            ]
        return tuple(main)

    def prepare(self):
        kind, bit = self.step = self.plan.pop(0)
        if kind == "gather":
            total = self.merged()
            self.gathered = (total, bit)
            return total
        mine = own_bit(kind, bit)
        if kind == "ctx":
            total = self.merged()
            self.kept = pick(total, mine, total.ndim - 3)
            return pick(total, 1 - mine, total.ndim - 3)
        send = self.added(
            [term.take(1 - mine) for term in self.terms],
            [item.take(1 - mine) for item in self.received],
        )
        self.terms = [term.take(mine) for term in self.terms]
        self.received = [item.take(mine) for item in self.received]
        return send

    def exchange(self, send):
        kind, bit = self.step
        other = swap(send, "fsdp" if kind == "fsdp" else "ctx", bit)
        if kind == "fsdp":
            self.received.append(Part(other))
        else:
            self.pending = other

    def result(self):
        total = self.merged()
        return total.reshape(-1, total.shape[-1])


class Gathering(Reduction):
    def __init__(self, rows):
        super().__init__([Ready(rows, 1)], "gather")

    def merged(self):
        return super().merged() if self.gathered is not None else self.shard()


def finish(item):
    while item.plan:
        advance([item])
    return item.shard()


def advance(sums, *main):
    if main:
        for item in sums:
            main = item.settle(main)
    sends = [item.prepare() for item in sums]
    held = lax.optimization_barrier(tuple(sends) + tuple(main))
    for item, send in zip(sums, held):
        item.exchange(send)
    main = held[len(sums) :]
    return main[0] if len(main) == 1 else main


def weighed(weight, grad):
    return jnp.sum(weight.astype(jnp.float32) * grad[:, : weight.shape[1]], axis=1)


def body(tokens, encoded, cotangent, w_self, w_cross, w_ffn, gains, table, bucket_ids, block_order):
    row_count = tokens.shape[1]
    model_width = tokens.shape[2]
    head_count = table.shape[1]
    head_size = model_width // head_count
    hidden_units = w_ffn.shape[1] // 3
    block = row_count // 2
    seq_length = bucket_ids.shape[0]
    steps = seq_length // block
    ctx_place = lax.axis_index("ctx")
    fsdp_size = lax.axis_size("fsdp")
    small = jnp.concatenate([gains.reshape(1, -1), table.reshape(1, -1)], axis=1)
    far_small = far_rows(small)
    held_self = far_rows(w_self)
    held_self = near_rows(
        [(after(piece, *[other for other, _ in far_small[1:]]), at) for piece, at in held_self]
    )
    small_held = near_rows(far_small)
    small = jnp.zeros((fsdp_size, small.shape[1]), small.dtype)
    for piece, at in small_held:
        small = lax.dynamic_update_slice_in_dim(small, piece, at, 0)
    gain_rows = jnp.transpose(
        small[:, : gains.size].reshape((fsdp_size,) + gains.shape), (1, 0, 2)
    ).reshape(gains.shape[0], -1)
    table_rows = small[:, gains.size :].reshape(-1, head_count)
    token_rows = lax.all_gather(tokens[0], "ctx", axis=0, tiled=True)
    encoder_sum = Gathering(encoded[0])
    advance([encoder_sum])
    held_cross = far_rows(after(w_cross, small, *[piece for piece, _ in held_self[1:]]))
    held_ffn = far_rows(after(w_ffn, *[piece for piece, _ in held_cross[1:]]))
    whole_self = place_rows([piece for piece, _ in held_self], [at for _, at in held_self])
    encoder_sum.pending = after(encoder_sum.pending, whole_self[:8, :LANES])
    advance([encoder_sum])
    gain_float = gain_rows.astype(jnp.float32)
    bucket_count = table_rows.shape[0]
    in_bucket = (
        bucket_ids[None, :] == jnp.arange(bucket_count, dtype=jnp.int32)[:, None]
    ).astype(jnp.float32)
    by_distance = lax.dot_general(
        table_rows.astype(jnp.float32),
        in_bucket,
        (((0,), (0,)), ((), ())),
        precision=lax.Precision.HIGHEST,
    )
    tiles = bias_tiles(
        after(distance_rows(by_distance, block), whole_self), LANES // head_size
    )
    own_blocks = lax.dynamic_slice_in_dim(block_order, 2 * ctx_place, 2)
    apart = own_blocks[:, None] - block_order[None, :]
    places = jnp.where(apart < 0, steps, apart).astype(jnp.int32).reshape(-1)

    inputs = tokens[0].astype(jnp.float32)
    gain_first = after(gain_float[0], tiles)
    normed_all = rounded(row_norm(token_rows.astype(jnp.float32), gain_first))
    normed_all = advance([encoder_sum], normed_all)
    normed_one = rounded(row_norm(inputs, gain_float[0]))
    queries = rounded(dot(normed_one, whole_self[:, :model_width]))
    key_values = rounded(dot(normed_all, whole_self[:, model_width : 3 * model_width]))
    held_cross = near_rows([(after(piece, normed_one), at) for piece, at in held_cross])
    attended, weights, inverses = attention_forward(queries, key_values, head_size, tiles, places)
    held_cross = [(after(piece, attended), at) for piece, at in held_cross]
    whole_cross = place_rows([piece for piece, _ in held_cross], [at for _, at in held_cross])
    after_one = inputs + dot(attended, whole_self[:, 3 * model_width :])
    normed_two = rounded(row_norm(after_one, gain_float[1]))
    cross_query = rounded(dot(normed_two, whole_cross[:, :model_width]))
    cross_query = encoder_sum.settle((cross_query,))[0]
    while encoder_sum.plan:
        cross_query = advance([encoder_sum], cross_query)
    encoder_all = encoder_sum.result()
    encoder_kv = rounded(dot(encoder_all, whole_cross[:, model_width : 3 * model_width]))
    held_ffn = near_rows([(after(piece, encoder_kv), at) for piece, at in held_ffn])
    cross_rows, cross_weights, cross_inverses = attention_forward(
        cross_query, encoder_kv, head_size
    )
    held_ffn = [(after(piece, cross_rows), at) for piece, at in held_ffn]
    whole_ffn = place_rows([piece for piece, _ in held_ffn], [at for _, at in held_ffn])
    after_two = after_one + dot(cross_rows, whole_cross[:, 3 * model_width :])
    normed_three = rounded(row_norm(after_two, gain_float[2]))
    gate_up = dot(normed_three, whole_ffn[:, : 2 * hidden_units])
    mixed_float, gated_back = jax.vjp(gated_gelu, gate_up)
    mixed_rows = rounded(mixed_float)
    output = rounded(after_two + dot_t(mixed_rows, whole_ffn[:, 2 * hidden_units :]))

    grad_branch_three = cotangent[0]
    grad_after_two = grad_branch_three.astype(jnp.float32)
    grad_mixed = dot(grad_branch_three, whole_ffn[:, 2 * hidden_units :])
    grad_gate_up = rounded(gated_back(grad_mixed)[0])
    grad_normed_three = dot_t(grad_gate_up, whole_ffn[:, : 2 * hidden_units])
    ffn_sum = Reduction(
        [
            Product(normed_three, grad_gate_up, fsdp_size),
            Product(grad_branch_three, mixed_rows, fsdp_size),
        ],
        "fsdp",
    )
    grad_normed_three = advance([ffn_sum], grad_normed_three)
    norm_part = jax.vjp(row_norm, after_two, gain_float[2])[1](grad_normed_three)[0]
    grad_after_one = grad_after_two + norm_part
    grad_branch_two = rounded(grad_after_one)
    grad_cross_rows = rounded(dot_t(grad_branch_two, whole_cross[:, 3 * model_width :]))
    grad_cross_rows = advance([ffn_sum], grad_cross_rows)
    grad_cross_query, encoder_full = attention_backward(
        cross_query, encoder_kv, grad_cross_rows, cross_rows, cross_weights, cross_inverses,
        head_size, False,
    )
    grad_normed_two = dot_t(grad_cross_query, whole_cross[:, :model_width])
    norm_part = jax.vjp(row_norm, after_one, gain_float[1])[1](grad_normed_two)[0]
    grad_inputs_one = grad_after_one + norm_part
    grad_branch_one = rounded(grad_inputs_one)
    grad_attended = rounded(dot_t(grad_branch_one, whole_self[:, 3 * model_width :]))
    cross_sum = Reduction(
        [
            Product(normed_two, grad_cross_query, fsdp_size),
            Product(encoder_all, encoder_full[0], fsdp_size),
            Product(encoder_all, encoder_full[1], fsdp_size),
            Product(cross_rows, grad_branch_two, fsdp_size),
        ],
        "fsdp",
    )
    grad_encoder_part = back_to_rows(encoder_full, whole_cross, model_width)
    encoder_back = Reduction([Ready(grad_encoder_part, 1)], "ctx")
    grad_attended = advance([cross_sum, encoder_back], grad_attended)
    grad_query, grad_keys, distance_sums = attention_backward(
        queries, key_values, grad_attended, attended, weights, inverses, head_size, True
    )
    self_sum = Reduction(
        [
            Product(normed_one, grad_query, fsdp_size),
            Product(normed_all, grad_keys[0], fsdp_size),
            Product(normed_all, grad_keys[1], fsdp_size),
            Product(attended, grad_branch_one, fsdp_size),
        ],
        "fsdp",
    )
    grad_query, grad_keys, distance_sums = advance(
        [self_sum], grad_query, grad_keys, distance_sums
    )
    ffn_shard, grad_query, grad_keys, distance_sums = lax.optimization_barrier(
        (finish(ffn_sum), grad_query, grad_keys, distance_sums)
    )
    grad_query, grad_keys = advance([cross_sum], grad_query, grad_keys)
    ffn_shard = lax.psum_scatter(ffn_shard, "ctx", scatter_dimension=0, tiled=True)
    key_weights = whole_self[:, model_width : 2 * model_width]
    value_weights = whole_self[:, 2 * model_width : 3 * model_width]
    grad_normed_part = back_to_rows(grad_keys, whole_self, model_width)
    token_sum = Reduction([Ready(grad_normed_part, 1)], "ctx")
    distance_sums = advance([token_sum], distance_sums)
    distance_sums = advance([self_sum], distance_sums)
    distance_sums = cross_sum.settle((distance_sums,))[0]
    distance_sums = advance([encoder_back], distance_sums)
    in_place = (places[None, :] == jnp.arange(steps, dtype=jnp.int32)[:, None]).astype(jnp.float32)
    distance_sums = jnp.einsum(
        "sp,hpw->hsw", in_place, distance_sums, precision=lax.Precision.HIGHEST
    )
    grad_table = lax.dot_general(
        in_bucket,
        by_distance_sums(distance_sums, block),
        (((1,), (1,)), ((), ())),
        precision=lax.Precision.HIGHEST,
    )
    grad_normed_query = dot_t(grad_query, whole_self[:, :model_width])
    cross_rest = Reduction([Ready(finish(cross_sum), 1)], "ctx", "gather")
    grad_table = advance([cross_rest], grad_table)
    for bit in range(bit_count("fsdp")):
        grad_table = grad_table + swap(grad_table, "fsdp", bit)
    table_columns = jnp.pad(
        lax.dynamic_slice_in_dim(
            grad_table, lax.axis_index("fsdp") * table.shape[0], table.shape[0], 0
        ),
        ((0, gains.shape[1] - table.shape[0]), (0, LANES - head_count)),
    )
    rest = jnp.concatenate([finish(self_sum), rounded(table_columns)], axis=1)
    rest = advance([token_sum], rest)
    ffn_shard, rest = lax.optimization_barrier((ffn_shard, rest))
    ffn_rows = lax.all_gather(ffn_shard, "ctx", axis=0, tiled=True)
    rest_sum = Reduction([Ready(rest, 1)], "ctx", "gather")
    advance([rest_sum])
    advance([cross_rest, encoder_back])
    ahead = [token_sum, encoder_back, cross_rest]
    while rest_sum.plan:
        ahead = [item for item in ahead if item.plan]
        if ahead:
            rest_sum.pending = advance(ahead, rest_sum.pending)
        if len(rest_sum.plan) == bit_count("ctx"):
            rest_sum.pending, ffn_rows = lax.optimization_barrier((rest_sum.pending, ffn_rows))
        advance([rest_sum])
    while any(item.plan for item in ahead):
        advance([item for item in ahead if item.plan])
    grad_normed_one = grad_normed_query + token_sum.result().astype(jnp.float32)
    norm_part = jax.vjp(row_norm, inputs, gain_float[0])[1](grad_normed_one)[0]
    grad_tokens = rounded(grad_inputs_one + norm_part)
    grad_encoded = encoder_back.result()
    ffn_grad = ffn_rows.astype(jnp.float32)
    cross_grad = cross_rest.result().astype(jnp.float32)
    rest = rest_sum.result().astype(jnp.float32)
    self_grad = rest[:, : 4 * model_width]
    table_own = rest[: table.shape[0], 4 * model_width : 4 * model_width + head_count]
    gain_own = jnp.stack(
        [
            weighed(w_self[:, : 3 * model_width], self_grad),
            weighed(w_cross[:, :model_width], cross_grad),
            weighed(w_ffn[:, : 2 * hidden_units], ffn_grad),
        ]
    ) / gains.astype(jnp.float32)
    return (
        output[None],
        grad_tokens[None],
        grad_encoded[None],
        self_grad,
        cross_grad,
        ffn_grad,
        gain_own,
        table_own,
    )


def solution(mesh):
    in_specs = (
        P("fsdp", "ctx", None),
        P("fsdp", "ctx", None),
        P("fsdp", "ctx", None),
        P("fsdp", None),
        P("fsdp", None),
        P("fsdp", None),
        P(None, "fsdp"),
        P("fsdp", None),
        P(),
        P(),
    )
    out_specs = (
        P("fsdp", "ctx", None),
        P("fsdp", "ctx", None),
        P("fsdp", "ctx", None),
        P("fsdp", None),
        P("fsdp", None),
        P("fsdp", None),
        P(None, "fsdp"),
        P("fsdp", None),
    )
    return jax.shard_map(body, mesh=mesh, in_specs=in_specs, out_specs=out_specs, check_vma=False)
```
